32 devices in a mesh: dp: 2 (over x), expert: 16 (over z, y, core).
Axes of the slice: x: 2, y: 2, z: 4, core: 2. Of those that a mesh axis runs over, the one named last changes fastest.
Arguments:
- tokens: bfloat16 [4096, 2048], P(('dp', 'expert')), may hold values from -6 to 6
- expert_ids: int32 [4096], P(('dp', 'expert')), may hold values from 0 to 15
- gate: float32 [4096], P(('dp', 'expert')), may hold values from 0.2 to 1
- cotangent: bfloat16 [4096, 2048], P(('dp', 'expert')), may hold values from -6 to 6
- w_up: bfloat16 [16, 2048, 768], P('expert'), may hold values from -0.125 to 0.125
- w_down: bfloat16 [16, 768, 2048], P('expert'), may hold values from -0.21875 to 0.21875
Outputs:
- layer_out: bfloat16 [4096, 2048], P(('dp', 'expert'))
- token_grad: bfloat16 [4096, 2048], P(('dp', 'expert'))
- up_grad: float32 [16, 2048, 768], P('expert', 'dp')
- down_grad: float32 [16, 768, 2048], P('expert', None, 'dp')
The draws below stay inside these ranges and needn't reach their ends.
All inputs are finite; a program needn't handle non-finite values.
Results may differ from the reference program's by a relative error of at most 0.013.
Values may be sent and summed in bfloat16 or wider, within the bound.
A program may use at most 64 MiB of HBM per device.

```python
import math
import jax
import jax.numpy as jnp
import numpy as np
from jax import lax

D = 2048
FF = 768
TOK_DEV = 128
EXPERTS = 16
CAPACITY = 8
TOKENS = 4096
N_DP = 2
N_EXPERT = 16


def set_ends(entries, rng, least, top_value):
    shape = entries.shape
    index_at = [jax.random.randint(jax.random.fold_in(rng, axis), (), 0, shape[axis]) for axis in range(len(shape))]
    entries = entries.at[tuple(index_at)].set(least)
    longest = shape.index(max(shape))
    index_at[longest] = (index_at[longest] + 1) % shape[longest]
    return entries.at[tuple(index_at)].set(top_value)


def levels(rng, shape, shards, least, high):
    level = 1.0
    for dim, shards_of in shards:
        draws = jax.random.uniform(jax.random.fold_in(jax.random.fold_in(rng, 6), dim), (shards_of,), jnp.float32, least / len(shards), high / len(shards))
        level = level * jnp.repeat(jnp.exp(draws), shape[dim] // shards_of).reshape((-1,) + (1,) * (len(shape) - 1 - dim))
    return level


def rank_bounds(count, lean):
    portions = [(1 << 20) // math.isqrt(rank ** lean) + 1 for rank in range(1, count + 1)]
    deviation = 1 + sum(portions) // (1 << 30)
    return np.cumsum(np.array([max(1, weight // deviation) for weight in portions]))


def ranked_ids(own_key, shape, amount, skew):
    grid = rank_bounds(amount, skew)
    lot = jax.random.randint(jax.random.fold_in(own_key, 1), shape, 0, int(grid[amount - 1]))
    rank = jnp.searchsorted(jnp.asarray(grid, jnp.int32), lot, side="right")
    return jax.random.permutation(jax.random.fold_in(own_key, 2), amount)[rank].astype(jnp.int32)


def bell_draw(rng, dims, width, most, shards=(), kind=jnp.bfloat16):
    entries = width * jax.random.normal(rng, dims, jnp.float32)
    if shards:
        entries = entries * levels(rng, dims, shards, -0.22, 0.18)
    return jnp.clip(entries, -most, most).astype(kind)


def setup_inputs(seed: int = 0) -> dict:
    key_list = jax.random.split(jax.random.key(seed), 7)
    return {
        "tokens": bell_draw(key_list[0], (TOKENS, D), 1.0, 6.0, ((0, 32),)),
        "expert_ids": set_ends(ranked_ids(key_list[1], (TOKENS,), EXPERTS, 2), jax.random.fold_in(key_list[1], 3), 0, EXPERTS - 1).astype(jnp.int32),
        "gate": jnp.clip(0.2 + 0.8 * jax.random.uniform(key_list[2], (TOKENS,), jnp.float32) ** levels(key_list[2], (TOKENS,), ((0, 32),), -0.2, 0.2), 0.2, 1.0),
        "cotangent": bell_draw(key_list[3], (TOKENS, D), 1.0, 6.0, ((0, 32),)),
        "w_up": bell_draw(key_list[4], (EXPERTS, D, FF), D ** -0.5, 0.125, ((0, 16),)),
        "w_down": bell_draw(key_list[5], (EXPERTS, FF, D), FF ** -0.5, 0.21875, ((0, 16),)),
    }


def reference(tokens, expert_ids, gate, cotangent, w_up, w_down):
    block_count = N_DP * N_EXPERT
    id_blocks = expert_ids.reshape(block_count, TOK_DEV)
    onehot = (id_blocks[:, :, None] == jnp.arange(EXPERTS, dtype=jnp.int32)[None, None, :]).astype(jnp.int32)
    row_rank = jnp.sum((jnp.cumsum(onehot, axis=1) - onehot) * onehot, axis=2)
    kept = row_rank < CAPACITY
    source = (jnp.arange(block_count, dtype=jnp.int32) % N_EXPERT)[:, None]
    per_expert = N_EXPERT * CAPACITY
    slot_total = EXPERTS * per_expert
    target = jnp.where(kept, id_blocks * per_expert + source * CAPACITY + row_rank, slot_total).astype(jnp.int32)
    scaled = (gate[:, None] * cotangent.astype(jnp.float32)).astype(jnp.bfloat16)
    group_rows = N_EXPERT * TOK_DEV
    w_in = w_up.astype(jnp.float32)
    w_out = w_down.astype(jnp.float32)

    def one_group(totals, inputs):
        group_tokens, group_scaled, group_target = inputs
        live = group_target < slot_total
        slot_x = jnp.zeros((slot_total, D), jnp.bfloat16).at[group_target].set(group_tokens, mode="drop")
        slot_c = jnp.zeros((slot_total, D), jnp.bfloat16).at[group_target].set(group_scaled, mode="drop")
        slot_x = slot_x.reshape(EXPERTS, per_expert, D).astype(jnp.float32)
        slot_c = slot_c.reshape(EXPERTS, per_expert, D).astype(jnp.float32)
        pre_act = jnp.einsum("erd,edf->erf", slot_x, w_in)
        hidden = jax.nn.silu(pre_act).astype(jnp.bfloat16)
        expert_out = jnp.einsum("erf,efd->erd", hidden.astype(jnp.float32), w_out).astype(jnp.bfloat16)
        back = jnp.einsum("erd,efd->erf", slot_c, w_out)
        sigma = jax.nn.sigmoid(pre_act)
        grad_pre = (back * sigma * (1.0 + pre_act * (1.0 - sigma))).astype(jnp.bfloat16)
        slot_grad = jnp.einsum("erf,edf->erd", grad_pre.astype(jnp.float32), w_in).astype(jnp.bfloat16)
        up_part = jnp.einsum("erd,erf->edf", slot_x, grad_pre.astype(jnp.float32)).astype(jnp.bfloat16)
        down_part = jnp.einsum("erf,erd->efd", hidden.astype(jnp.float32), slot_c).astype(jnp.bfloat16)
        index = jnp.minimum(group_target, slot_total - 1)
        out_rows = jnp.take(expert_out.reshape(slot_total, D), index, axis=0)
        grad_rows = jnp.take(slot_grad.reshape(slot_total, D), index, axis=0)
        out_rows = jnp.where(live[:, None], out_rows, jnp.zeros_like(out_rows))
        grad_rows = jnp.where(live[:, None], grad_rows, jnp.zeros_like(grad_rows))
        totals = (totals[0] + up_part.astype(jnp.float32), totals[1] + down_part.astype(jnp.float32))
        return totals, (out_rows, grad_rows)

    start = (jnp.zeros((EXPERTS, D, FF), jnp.float32), jnp.zeros((EXPERTS, FF, D), jnp.float32))
    inputs = (tokens.reshape(N_DP, group_rows, D), scaled.reshape(N_DP, group_rows, D), target.reshape(N_DP, group_rows))
    totals, rows = lax.scan(one_group, start, inputs)
    expert_out = rows[0].reshape(TOKENS, D)
    token_grad = rows[1].reshape(TOKENS, D)
    layer_out = (gate[:, None] * expert_out.astype(jnp.float32)).astype(jnp.bfloat16)
    inverse = 1.0 / N_DP
    return layer_out, token_grad, totals[0] * inverse, totals[1] * inverse
```

```python
import functools

import jax
import jax.numpy as jnp
from jax import lax
from jax.experimental import pallas as pl
from jax.experimental.pallas import tpu as pltpu
from jax.sharding import PartitionSpec as P

MESH = pl.DeviceIdType.MESH
F32 = jnp.float32
BF16 = jnp.bfloat16
CHUNK = 4


def column(row):
    t = row.shape[1]
    eye = lax.broadcasted_iota(jnp.int32, (t, t), 0) == lax.broadcasted_iota(jnp.int32, (t, t), 1)
    return jnp.sum(jnp.where(eye, row, jnp.zeros_like(row)), axis=1, keepdims=True)


def place(ids, me, n, capacity):
    t = ids.shape[1]
    onehot = lax.broadcasted_iota(jnp.int32, (n, t), 0) == ids
    before = lax.broadcasted_iota(jnp.int32, (t, t), 0) < lax.broadcasted_iota(jnp.int32, (t, t), 1)
    counts = jnp.dot(
        onehot.astype(F32).astype(BF16), before.astype(F32).astype(BF16), preferred_element_type=F32
    )
    rank = jnp.sum(jnp.where(onehot, counts, 0.0), axis=0, keepdims=True).astype(jnp.int32)
    offset = ids - me
    offset = jnp.where(offset < 0, offset + n, offset)
    return offset, rank, rank < capacity


def exchange_kernel(
    n, groups, capacity, pad, ids_ref, gate_ref, tokens_ref, cot_ref, wup_hbm, wdn_hbm,
    back_ref, a_all, hg_all, wup, wdn, send, recv, ret, hg,
    w_sem, send_sem, recv_sem, rsend_sem, rrecv_sem, self_sem,
    a_sem, h_sem, asend_sem, arecv_sem, hsend_sem, hrecv_sem,
):
    dp = lax.axis_index("dp")
    me = lax.axis_index("expert")
    width = tokens_ref.shape[1]
    units = wup.shape[1]
    cols = width // groups
    chunks = n // CHUNK
    wcopy = [
        pltpu.make_async_copy(wup_hbm, wup, w_sem.at[0]),
        pltpu.make_async_copy(wdn_hbm, wdn, w_sem.at[1]),
    ]
    for copy in wcopy:
        copy.start()

    barrier = pltpu.get_barrier_semaphore()

    @pl.loop(1, n)
    def _(k):
        pl.semaphore_signal(
            barrier, inc=1, device_id=(dp, lax.rem(me + k, n)), device_id_type=MESH
        )

    @pl.loop(1, groups)
    def _(d):
        pl.semaphore_signal(
            barrier, inc=1, device_id=(lax.rem(dp + d, groups), me), device_id_type=MESH
        )

    offset, rank, kept = place(ids_ref[...], me, n, capacity)
    t = tokens_ref.shape[0]
    target = jnp.where(kept, offset * pad + rank, -1)
    select = (lax.broadcasted_iota(jnp.int32, (n * pad, t), 0) == target).astype(F32).astype(BF16)
    scaled = (column(gate_ref[...]) * cot_ref[...].astype(F32)).astype(BF16)
    step = 512 if width % 512 == 0 else width
    for at in range(0, width, step):
        x = jnp.dot(select, tokens_ref[:, at : at + step], preferred_element_type=F32)
        c = jnp.dot(select, scaled[:, at : at + step], preferred_element_type=F32)
        both = jnp.concatenate([x.reshape(n, pad, step), c.reshape(n, pad, step)], axis=1)
        both = both.astype(BF16)
        send[:, :, at : at + step] = both
        recv[0, :, at : at + step] = both[0]

    pl.semaphore_wait(barrier, n - 1 + groups - 1)

    def forth(k):
        return pltpu.make_async_remote_copy(
            src_ref=send.at[k], dst_ref=recv.at[k], send_sem=send_sem.at[k],
            recv_sem=recv_sem.at[k], device_id=(dp, lax.rem(me + k, n)), device_id_type=MESH,
        )

    def home(k):
        return pltpu.make_async_remote_copy(
            src_ref=ret.at[k], dst_ref=back_ref.at[k], send_sem=rsend_sem.at[k],
            recv_sem=rrecv_sem.at[k], device_id=(dp, lax.rem(me + n - k, n)), device_id_type=MESH,
        )

    def a_local(c):
        return pltpu.make_async_copy(
            recv.at[pl.ds(c * CHUNK, CHUNK), :, pl.ds(pl.multiple_of(dp * cols, 128), cols)],
            a_all.at[0, pl.ds(c * CHUNK, CHUNK)], a_sem.at[c],
        )

    def h_local(c):
        return pltpu.make_async_copy(
            hg.at[pl.ds(c * CHUNK, CHUNK)], hg_all.at[0, pl.ds(c * CHUNK, CHUNK)], h_sem.at[c]
        )

    def a_remote(c, d):
        peer = lax.rem(dp + d, groups)
        return pltpu.make_async_remote_copy(
            src_ref=recv.at[
                pl.ds(c * CHUNK, CHUNK), :, pl.ds(pl.multiple_of(peer * cols, 128), cols)
            ],
            dst_ref=a_all.at[d, pl.ds(c * CHUNK, CHUNK)], send_sem=asend_sem.at[d, c],
            recv_sem=arecv_sem.at[d, c], device_id=(peer, me), device_id_type=MESH,
        )

    def h_remote(c, d):
        peer = lax.rem(dp + d, groups)
        return pltpu.make_async_remote_copy(
            src_ref=hg.at[pl.ds(c * CHUNK, CHUNK)],
            dst_ref=hg_all.at[d, pl.ds(c * CHUNK, CHUNK)], send_sem=hsend_sem.at[d, c],
            recv_sem=hrecv_sem.at[d, c], device_id=(peer, me), device_id_type=MESH,
        )

    @pl.loop(1, n)
    def _(i):
        forth(n - i).start()

    for copy in wcopy:
        copy.wait()

    rows = CHUNK * pad
    nt = (((1,), (1,)), ((), ()))

    @pl.loop(0, chunks)
    def _(i):
        c = chunks - 1 - i

        @pl.loop(0, CHUNK)
        def _(j):
            k = c * CHUNK + j

            @pl.when(k > 0)
            def _():
                forth(k).wait_recv()

        a_local(c).start()

        @pl.loop(1, groups)
        def _(d):
            a_remote(c, d).start()

        a = recv[pl.ds(c * CHUNK, CHUNK)].reshape(2 * rows, width)
        pre = jnp.dot(a, wup[...], preferred_element_type=F32)
        grad = lax.dot_general(a, wdn[...], nt, preferred_element_type=F32)
        pre = pre.reshape(CHUNK, 2, pad, units)[:, 0]
        grad = grad.reshape(CHUNK, 2, pad, units)[:, 1]
        sigma = 1.0 / (1.0 + jnp.exp(-pre))
        hidden = pre * sigma
        grad = grad * sigma * (1.0 + pre * (1.0 - sigma))
        hg[pl.ds(c * CHUNK, CHUNK)] = jnp.concatenate([grad, hidden], axis=1).astype(BF16)
        h_local(c).start()

        @pl.loop(1, groups)
        def _(d):
            h_remote(c, d).start()

        hidden = hidden.reshape(rows, units).astype(BF16)
        grad = grad.reshape(rows, units).astype(BF16)
        for at in range(0, width, step):
            out = jnp.dot(hidden, wdn[:, at : at + step], preferred_element_type=F32)
            tok = lax.dot_general(grad, wup[at : at + step, :], nt, preferred_element_type=F32)
            both = jnp.concatenate(
                [tok.reshape(CHUNK, pad, step), out.reshape(CHUNK, pad, step)], axis=1
            )
            ret[pl.ds(c * CHUNK, CHUNK), :, at : at + step] = both.astype(BF16)

        @pl.loop(0, CHUNK)
        def _(j):
            k = c * CHUNK + j

            @pl.when(k > 0)
            def _():
                home(k).start()

    own = pltpu.make_async_copy(ret.at[0], back_ref.at[0], self_sem)
    own.start()

    @pl.loop(0, chunks)
    def _(c):
        a_local(c).wait()
        h_local(c).wait()

        @pl.loop(1, groups)
        def _(d):
            a_remote(c, d).wait()
            h_remote(c, d).wait()

    @pl.loop(1, n)
    def _(k):
        forth(k).wait_send()
        home(k).wait()

    own.wait()


def exchange(n, groups, capacity, pad, ids, gate, tokens, cot, wup, wdn):
    width = tokens.shape[1]
    units = wup.shape[1]
    chunks = n // CHUNK
    vmem = pl.BlockSpec(memory_space=pltpu.VMEM)
    hbm = pl.BlockSpec(memory_space=pl.ANY)
    dma = pltpu.SemaphoreType.DMA
    block = (n, 2 * pad, width)
    return pl.pallas_call(
        functools.partial(exchange_kernel, n, groups, capacity, pad),
        out_shape=(
            jax.ShapeDtypeStruct(block, BF16),
            jax.ShapeDtypeStruct((groups, n, 2 * pad, width // groups), BF16),
            jax.ShapeDtypeStruct((groups, n, 2 * pad, units), BF16),
        ),
        in_specs=[vmem, vmem, vmem, vmem, hbm, hbm],
        out_specs=(hbm, hbm, hbm),
        scratch_shapes=[
            pltpu.VMEM(wup.shape, BF16), pltpu.VMEM(wdn.shape, BF16),
            pltpu.VMEM(block, BF16), pltpu.VMEM(block, BF16), pltpu.VMEM(block, BF16),
            pltpu.VMEM((n, 2 * pad, units), BF16),
            dma((2,)), dma((n,)), dma((n,)), dma((n,)), dma((n,)), dma,
            dma((chunks,)), dma((chunks,)),
            dma((groups, chunks)), dma((groups, chunks)),
            dma((groups, chunks)), dma((groups, chunks)),
        ],
        compiler_params=pltpu.CompilerParams(
            collective_id=0, has_side_effects=True, vmem_limit_bytes=44 * 2**20
        ),
        name="expert_exchange",
    )(ids, gate, tokens, cot, wup, wdn)


def finish_kernel(
    n, capacity, pad, inverse, me_ref, ids_ref, gate_ref, back_ref, a_ref, hg_ref,
    out_ref, tok_ref, up_ref, down_ref,
):
    g = pl.program_id(1)

    @pl.when(g == 0)
    def _():
        offset, rank, kept = place(ids_ref[...], me_ref[0, 0], n, capacity)
        target = column(jnp.where(kept, offset * (2 * pad) + rank, -2 * pad))
        t = target.shape[0]
        slot = lax.broadcasted_iota(jnp.int32, (t, n * 2 * pad), 1)
        pick_tok = (slot == target).astype(F32).astype(BF16)
        pick_out = (slot == target + pad).astype(F32).astype(BF16)
        rows = back_ref[...]
        tok_ref[...] = jnp.dot(pick_tok, rows, preferred_element_type=F32).astype(BF16)
        out = jnp.dot(pick_out, rows, preferred_element_type=F32)
        out_ref[...] = (column(gate_ref[...]) * out).astype(BF16)

    a = a_ref[0]
    hg = hg_ref[0]
    first = lax.rem(lax.broadcasted_iota(jnp.int32, hg.shape, 0), 2 * pad) < pad
    zero = jnp.zeros_like(hg)
    tn = (((0,), (0,)), ((), ()))
    up = lax.dot_general(a, jnp.where(first, hg, zero), tn, preferred_element_type=F32) * inverse
    down = lax.dot_general(jnp.where(first, zero, hg), a, tn, preferred_element_type=F32) * inverse

    @pl.when(g == 0)
    def _():
        up_ref[...] = up
        down_ref[...] = down

    @pl.when(g > 0)
    def _():
        up_ref[...] += up
        down_ref[...] += down


def finish(n, groups, capacity, pad, me, ids, gate, back, a_all, hg_all):
    rows, cols = a_all.shape[1], a_all.shape[2]
    units = hg_all.shape[2]
    t = ids.shape[1]
    width = back.shape[1]
    tile = 256 if cols % 256 == 0 else cols
    tiles = cols // tile
    wide = width // tiles
    whole = pl.BlockSpec((1, t), lambda j, g: (0, 0))
    return pl.pallas_call(
        functools.partial(finish_kernel, n, capacity, pad, 1.0 / groups),
        grid=(tiles, groups),
        out_shape=(
            jax.ShapeDtypeStruct((t, width), BF16),
            jax.ShapeDtypeStruct((t, width), BF16),
            jax.ShapeDtypeStruct((cols, units), F32),
            jax.ShapeDtypeStruct((units, cols), F32),
        ),
        in_specs=[
            pl.BlockSpec(memory_space=pltpu.SMEM),
            whole,
            whole,
            pl.BlockSpec((rows, wide), lambda j, g: (0, j)),
            pl.BlockSpec((1, rows, tile), lambda j, g: (g, 0, j)),
            pl.BlockSpec((1, rows, units), lambda j, g: (g, 0, 0)),
        ],
        out_specs=(
            pl.BlockSpec((t, wide), lambda j, g: (0, j)),
            pl.BlockSpec((t, wide), lambda j, g: (0, j)),
            pl.BlockSpec((tile, units), lambda j, g: (j, 0)),
            pl.BlockSpec((units, tile), lambda j, g: (0, j)),
        ),
        compiler_params=pltpu.CompilerParams(vmem_limit_bytes=40 * 2**20),
        name="finish",
    )(me, ids, gate, back, a_all, hg_all)


def shards(tokens, expert_ids, gate, cotangent, w_up, w_down):
    t = tokens.shape[0]
    n = lax.axis_size("expert")
    groups = lax.axis_size("dp")
    capacity = t // n
    pad = -(-capacity // 8) * 8
    ids = expert_ids[None]
    gate = gate[None]
    back, a_all, hg_all = exchange(
        n, groups, capacity, pad, ids, gate, tokens, cotangent, w_up[0], w_down[0]
    )
    me = lax.axis_index("expert").astype(jnp.int32).reshape(1, 1)
    rows = n * 2 * pad
    out, tok, up, down = finish(
        n, groups, capacity, pad, me, ids, gate, back.reshape(rows, -1),
        a_all.reshape(groups, rows, -1), hg_all.reshape(groups, rows, -1),
    )
    return out, tok, up[None], down[None]


def solution(mesh):
    in_specs = (
        P(("dp", "expert"), None),
        P(("dp", "expert")),
        P(("dp", "expert")),
        P(("dp", "expert"), None),
        P("expert", None, None),
        P("expert", None, None),
    )
    out_specs = (
        P(("dp", "expert"), None),
        P(("dp", "expert"), None),
        P("expert", "dp", None),
        P("expert", None, "dp"),
    )
    return jax.shard_map(shards, mesh=mesh, in_specs=in_specs, out_specs=out_specs, check_vma=False)
```

```python
import functools
import math

import jax
import jax.numpy as jnp
from jax import lax
from jax.experimental import pallas as pl
from jax.experimental.pallas import tpu as pltpu
from jax.sharding import PartitionSpec as P

MESH = pl.DeviceIdType.MESH
F32 = jnp.float32
BF16 = jnp.bfloat16
CHUNK = 4


def column(row):
    t = row.shape[1]
    eye = lax.broadcasted_iota(jnp.int32, (t, t), 0) == lax.broadcasted_iota(jnp.int32, (t, t), 1)
    return jnp.sum(jnp.where(eye, row, jnp.zeros_like(row)), axis=1, keepdims=True)


def place(ids, me, n, capacity):
    t = ids.shape[1]
    onehot = lax.broadcasted_iota(jnp.int32, (n, t), 0) == ids
    before = lax.broadcasted_iota(jnp.int32, (t, t), 0) < lax.broadcasted_iota(jnp.int32, (t, t), 1)
    counts = jnp.dot(
        onehot.astype(F32).astype(BF16), before.astype(F32).astype(BF16), preferred_element_type=F32
    )
    rank = jnp.sum(jnp.where(onehot, counts, 0.0), axis=0, keepdims=True).astype(jnp.int32)
    offset = ids - me
    offset = jnp.where(offset < 0, offset + n, offset)
    return offset, rank, rank < capacity


def exchange_kernel(
    n, groups, capacity, pad, ids_hbm, gate_hbm, tokens_hbm, cot_hbm, wup_hbm, wdn_hbm,
    back_ref, up_out, down_out, pick_out,
    ids_ref, gate_ref, tokens_ref, cot_ref, wup, wdn, send, recv, ret, hg, a_all, hg_all,
    up_acc, down_acc, pick,
    in_sem, out_sem, send_sem, recv_sem, rsend_sem, rrecv_sem,
    asend_sem, arecv_sem, hsend_sem, hrecv_sem,
):
    dp = lax.axis_index("dp")
    me = lax.axis_index("expert")
    width = tokens_ref.shape[1]
    units = wup.shape[1]
    cols = width // groups
    chunks = n // CHUNK
    lead = chunks // 2 * CHUNK
    pairs = (
        (ids_hbm, ids_ref), (tokens_hbm, tokens_ref), (gate_hbm, gate_ref), (cot_hbm, cot_ref),
        (wup_hbm, wup), (wdn_hbm, wdn),
    )
    loads = [pltpu.make_async_copy(src, dst, in_sem.at[i]) for i, (src, dst) in enumerate(pairs)]
    for copy in loads:
        copy.start()

    barrier = pltpu.get_barrier_semaphore()

    @pl.loop(1, n)
    def _(k):
        pl.semaphore_signal(
            barrier, inc=1, device_id=(dp, lax.rem(me + k, n)), device_id_type=MESH
        )

    @pl.loop(1, groups)
    def _(d):
        pl.semaphore_signal(
            barrier, inc=1, device_id=(lax.rem(dp + d, groups), me), device_id_type=MESH
        )

    loads[0].wait()
    offset, rank, kept = place(ids_ref[...], me, n, capacity)
    t = tokens_ref.shape[0]
    target = jnp.where(kept, offset * pad + rank, -1)
    select = (lax.broadcasted_iota(jnp.int32, (n * pad, t), 0) == target).astype(F32).astype(BF16)
    for copy in loads[1:4]:
        copy.wait()
    scaled = (column(gate_ref[...]) * cot_ref[...].astype(F32)).astype(BF16)
    step = 512 if width % 512 == 0 else width
    for at in range(0, width, step):
        x = jnp.dot(select, tokens_ref[:, at : at + step], preferred_element_type=F32)
        c = jnp.dot(select, scaled[:, at : at + step], preferred_element_type=F32)
        both = jnp.concatenate([x.reshape(n, pad, step), c.reshape(n, pad, step)], axis=1)
        both = both.astype(BF16)
        send[:, :, at : at + step] = both
        recv[0, :, at : at + step] = both[0]

    pl.semaphore_wait(barrier, n - 1 + groups - 1)

    def forth(k):
        return pltpu.make_async_remote_copy(
            src_ref=send.at[k], dst_ref=recv.at[k], send_sem=send_sem.at[k],
            recv_sem=recv_sem.at[k], device_id=(dp, lax.rem(me + k, n)), device_id_type=MESH,
        )

    def home(k):
        return pltpu.make_async_remote_copy(
            src_ref=ret.at[k], dst_ref=back_ref.at[k], send_sem=rsend_sem.at[k],
            recv_sem=rrecv_sem.at[k], device_id=(dp, lax.rem(me + n - k, n)), device_id_type=MESH,
        )

    def a_remote(c, d):
        peer = lax.rem(dp + d, groups)
        return pltpu.make_async_remote_copy(
            src_ref=recv.at[
                pl.ds(c * CHUNK, CHUNK), :, pl.ds(pl.multiple_of(peer * cols, 128), cols)
            ],
            dst_ref=a_all.at[d - 1, pl.ds(c * CHUNK, CHUNK)], send_sem=asend_sem.at[d - 1, c],
            recv_sem=arecv_sem.at[d - 1, c], device_id=(peer, me), device_id_type=MESH,
        )

    def h_remote(c, d):
        peer = lax.rem(dp + d, groups)
        return pltpu.make_async_remote_copy(
            src_ref=hg.at[pl.ds(c * CHUNK, CHUNK)],
            dst_ref=hg_all.at[d - 1, pl.ds(c * CHUNK, CHUNK)], send_sem=hsend_sem.at[d - 1, c],
            recv_sem=hrecv_sem.at[d - 1, c], device_id=(peer, me), device_id_type=MESH,
        )

    for k in range(lead, lead + CHUNK):
        forth(k).start()
    for k in range(1, CHUNK):
        forth(k).start()

    slots = n * 2 * pad
    there = column(jnp.where(kept, offset * (2 * pad) + rank, -2 * pad))
    slot = lax.broadcasted_iota(jnp.int32, (t, slots), 1)
    pick[0] = (slot == there).astype(F32).astype(BF16)
    pick[1] = (slot == there + pad).astype(F32).astype(BF16)
    pick_copy = pltpu.make_async_copy(pick, pick_out, out_sem.at[0])
    pick_copy.start()

    for k in range(lead, lead + CHUNK // 2):
        forth(k).wait_send()

    @pl.loop(CHUNK, n)
    def _(k):
        @pl.when((k < lead) | (k >= lead + CHUNK))
        def _():
            forth(k).start()

    for copy in loads[4:]:
        copy.wait()

    rows = CHUNK * pad
    nt = (((1,), (1,)), ((), ()))

    @pl.loop(0, chunks)
    def _(i):
        c = jnp.where(i == 0, chunks // 2, jnp.where(i <= chunks // 2, i - 1, i))

        @pl.loop(0, CHUNK)
        def _(j):
            k = c * CHUNK + j

            @pl.when(k > 0)
            def _():
                forth(k).wait_recv()

        @pl.loop(1, groups)
        def _(d):
            a_remote(c, d).start()

        a = recv[pl.ds(c * CHUNK, CHUNK)].reshape(2 * rows, width)
        pre = jnp.dot(a, wup[...], preferred_element_type=F32)
        grad = lax.dot_general(a, wdn[...], nt, preferred_element_type=F32)
        pre = pre.reshape(CHUNK, 2, pad, units)[:, 0]
        grad = grad.reshape(CHUNK, 2, pad, units)[:, 1]
        sigma = 1.0 / (1.0 + jnp.exp(-pre))
        hidden = pre * sigma
        grad = grad * sigma * (1.0 + pre * (1.0 - sigma))
        hg[pl.ds(c * CHUNK, CHUNK)] = jnp.concatenate([grad, hidden], axis=1).astype(BF16)

        @pl.loop(1, groups)
        def _(d):
            h_remote(c, d).start()

        hidden = hidden.reshape(rows, units).astype(BF16)
        grad = grad.reshape(rows, units).astype(BF16)
        for at in range(0, width, step):
            out = jnp.dot(hidden, wdn[:, at : at + step], preferred_element_type=F32)
            tok = lax.dot_general(grad, wup[at : at + step, :], nt, preferred_element_type=F32)
            both = jnp.concatenate(
                [tok.reshape(CHUNK, pad, step), out.reshape(CHUNK, pad, step)], axis=1
            )
            ret[pl.ds(c * CHUNK, CHUNK), :, at : at + step] = both.astype(BF16)

        @pl.loop(0, CHUNK)
        def _(j):
            k = c * CHUNK + j

            @pl.when(k > 0)
            def _():
                home(k).start()

    own = pltpu.make_async_copy(ret.at[0], back_ref.at[0], out_sem.at[1])
    own.start()

    inverse = 1.0 / groups
    tile = 256 if cols % 256 == 0 else cols
    tn = (((0,), (0,)), ((), ()))

    def add_group(a_tile, grads, add):
        grads = grads.reshape(slots, units)
        first = lax.rem(lax.broadcasted_iota(jnp.int32, grads.shape, 0), 2 * pad) < pad
        zero = jnp.zeros_like(grads)
        grad = jnp.where(first, grads, zero)
        hidden = jnp.where(first, zero, grads)
        for at in range(0, cols, tile):
            a = a_tile(at).reshape(slots, tile)
            up = lax.dot_general(a, grad, tn, preferred_element_type=F32) * inverse
            down = lax.dot_general(hidden, a, tn, preferred_element_type=F32) * inverse
            if add:
                up += up_acc[at : at + tile, :]
                down += down_acc[:, at : at + tile]
            up_acc[at : at + tile, :] = up
            down_acc[:, at : at + tile] = down

    add_group(
        lambda at: recv[:, :, pl.ds(pl.multiple_of(dp * cols + at, 128), tile)], hg[...], False
    )

    @pl.loop(1, groups)
    def _(d):
        @pl.loop(0, chunks)
        def _(c):
            a_remote(c, d).wait_recv()
            h_remote(c, d).wait_recv()

        add_group(lambda at: a_all[d - 1, :, :, at : at + tile], hg_all[d - 1], True)

    up_copy = pltpu.make_async_copy(up_acc, up_out, out_sem.at[2])
    down_copy = pltpu.make_async_copy(down_acc, down_out, out_sem.at[3])
    up_copy.start()
    down_copy.start()

    @pl.loop(1, groups)
    def _(d):
        @pl.loop(0, chunks)
        def _(c):
            a_remote(c, d).wait_send()
            h_remote(c, d).wait_send()

    @pl.loop(1, n)
    def _(k):
        @pl.when((k < lead) | (k >= lead + CHUNK // 2))
        def _():
            forth(k).wait_send()

        home(k).wait()

    for copy in (pick_copy, own, up_copy, down_copy):
        copy.wait()


def nbytes(arrays):
    return sum(math.prod(shape) * jnp.dtype(kind).itemsize for shape, kind in arrays)


def exchange(n, groups, capacity, pad, ids, gate, tokens, cot, wup, wdn):
    t, width = tokens.shape
    units = wup.shape[1]
    cols = width // groups
    chunks = n // CHUNK
    hbm = pl.BlockSpec(memory_space=pltpu.HBM)
    anywhere = pl.BlockSpec(memory_space=pl.ANY)
    dma = pltpu.SemaphoreType.DMA
    block = (n, 2 * pad, width)
    buffers = [
        ((1, t), jnp.int32), ((1, t), F32), ((t, width), BF16), ((t, width), BF16),
        (wup.shape, BF16), (wdn.shape, BF16), (block, BF16), (block, BF16), (block, BF16),
        ((n, 2 * pad, units), BF16),
        ((groups - 1, n, 2 * pad, cols), BF16), ((groups - 1, n, 2 * pad, units), BF16),
        ((cols, units), F32), ((units, cols), F32), ((2, t, n * 2 * pad), BF16),
    ]
    results = [
        (block, BF16), ((cols, units), F32), ((units, cols), F32), ((2, t, n * 2 * pad), BF16),
    ]
    limit = nbytes(buffers) + 10 * 2**20
    near = limit + nbytes(results) < 52 * 2**20
    place_of = pltpu.VMEM if near else jax.ShapeDtypeStruct
    return pl.pallas_call(
        functools.partial(exchange_kernel, n, groups, capacity, pad),
        out_shape=tuple(place_of(shape, kind) for shape, kind in results),
        in_specs=[hbm] * 6,
        out_specs=(anywhere,) * 4,
        scratch_shapes=[pltpu.VMEM(shape, kind) for shape, kind in buffers]
        + [
            dma((6,)), dma((4,)), dma((n,)), dma((n,)), dma((n,)), dma((n,)),
            dma((groups - 1, chunks)), dma((groups - 1, chunks)),
            dma((groups - 1, chunks)), dma((groups - 1, chunks)),
        ],
        compiler_params=pltpu.CompilerParams(
            collective_id=0, has_side_effects=True, vmem_limit_bytes=limit
        ),
        name="expert_exchange",
    )(*(pltpu.with_memory_space_constraint(x, pltpu.HBM) for x in (ids, gate, tokens, cot, wup, wdn)))


def finish_kernel(
    gate_ref, pick_ref, back_ref, up_ref, down_ref, out_ref, tok_ref, up_out, down_out,
    out_buf, tok_buf, sem, row_sem,
):
    parts = sem.shape[1]
    copies = []
    for which, (src, dst) in enumerate(((up_ref, up_out), (down_ref, down_out))):
        size = src.shape[0] // parts
        for i in range(parts):
            rows = pl.ds(i * size, size)
            copies.append(pltpu.make_async_copy(src.at[rows], dst.at[rows], sem.at[which, i]))
    for copy in copies:
        copy.start()
    gate = column(gate_ref[...])
    width = out_ref.shape[1]
    step = 512 if width % 512 == 0 else width
    for i in range(width // step):
        at = pl.ds(i * step, step)
        rows = back_ref[:, at]
        tok = jnp.dot(pick_ref[0], rows, preferred_element_type=F32).astype(BF16)
        tok_buf[:, at] = tok
        out = jnp.dot(pick_ref[1], rows, preferred_element_type=F32)
        out_buf[:, at] = (gate * out).astype(BF16)
        for j, (src, dst) in enumerate(((tok_buf, tok_ref), (out_buf, out_ref))):
            copies.append(
                pltpu.make_async_copy(src.at[:, at], dst.at[:, at], row_sem.at[j, i])
            )
            copies[-1].start()
    for copy in copies:
        copy.wait()


def finish(gate, pick, back, up, down):
    t, width = gate.shape[1], back.shape[1]
    vmem = pl.BlockSpec(memory_space=pltpu.VMEM)
    anywhere = pl.BlockSpec(memory_space=pl.ANY)
    steps = width // 512 if width % 512 == 0 else 1
    return pl.pallas_call(
        finish_kernel,
        out_shape=(
            jax.ShapeDtypeStruct((t, width), BF16),
            jax.ShapeDtypeStruct((t, width), BF16),
            jax.ShapeDtypeStruct(up.shape, F32),
            jax.ShapeDtypeStruct(down.shape, F32),
        ),
        in_specs=[vmem, vmem, vmem, anywhere, anywhere],
        out_specs=(anywhere,) * 4,
        scratch_shapes=[
            pltpu.VMEM((t, width), BF16), pltpu.VMEM((t, width), BF16),
            pltpu.SemaphoreType.DMA((2, 4)), pltpu.SemaphoreType.DMA((2, steps)),
        ],
        compiler_params=pltpu.CompilerParams(vmem_limit_bytes=16 * 2**20),
        name="finish",
    )(gate, pick, back, up, down)


def shards(tokens, expert_ids, gate, cotangent, w_up, w_down):
    t = tokens.shape[0]
    n = lax.axis_size("expert")
    groups = lax.axis_size("dp")
    capacity = t // n
    pad = -(-capacity // 8) * 8
    gate = gate[None]
    back, up, down, pick = exchange(
        n, groups, capacity, pad, expert_ids[None], gate, tokens, cotangent, w_up[0], w_down[0]
    )
    out, tok, up, down = finish(gate, pick, back.reshape(n * 2 * pad, -1), up, down)
    return out, tok, up[None], down[None]


def solution(mesh):
    in_specs = (
        P(("dp", "expert"), None),
        P(("dp", "expert")),
        P(("dp", "expert")),
        P(("dp", "expert"), None),
        P("expert", None, None),
        P("expert", None, None),
    )
    out_specs = (
        P(("dp", "expert"), None),
        P(("dp", "expert"), None),
        P("expert", "dp", None),
        P("expert", None, "dp"),
    )
    return jax.shard_map(shards, mesh=mesh, in_specs=in_specs, out_specs=out_specs, check_vma=False)
```

```python
import functools
import math

import jax
import jax.numpy as jnp
from jax import lax
from jax.experimental import pallas as pl
from jax.experimental.pallas import tpu as pltpu
from jax.sharding import PartitionSpec as P

MESH = pl.DeviceIdType.MESH
F32 = jnp.float32
BF16 = jnp.bfloat16
CHUNK = 4


def column(row):
    t = row.shape[1]
    eye = lax.broadcasted_iota(jnp.int32, (t, t), 0) == lax.broadcasted_iota(jnp.int32, (t, t), 1)
    return jnp.sum(jnp.where(eye, row, jnp.zeros_like(row)), axis=1, keepdims=True)


def place(ids, me, n, capacity):
    t = ids.shape[1]
    onehot = lax.broadcasted_iota(jnp.int32, (n, t), 0) == ids
    before = lax.broadcasted_iota(jnp.int32, (t, t), 0) < lax.broadcasted_iota(jnp.int32, (t, t), 1)
    counts = jnp.dot(
        onehot.astype(F32).astype(BF16), before.astype(F32).astype(BF16), preferred_element_type=F32
    )
    rank = jnp.sum(jnp.where(onehot, counts, 0.0), axis=0, keepdims=True).astype(jnp.int32)
    offset = ids - me
    offset = jnp.where(offset < 0, offset + n, offset)
    return offset, rank, rank < capacity


def exchange_kernel(
    n, groups, capacity, pad, ids_hbm, gate_hbm, tokens_hbm, cot_hbm, wup_hbm, wdn_hbm,
    back_ref, up_out, down_out, pick_out,
    ids_ref, gate_ref, tokens_ref, cot_ref, scaled, wup, wdn, send, recv, ret, hg, a_all, hg_all,
    up_acc, down_acc, pick,
    in_sem, out_sem, send_sem, recv_sem, rsend_sem, rrecv_sem,
    asend_sem, arecv_sem, hsend_sem, hrecv_sem,
):
    dp = lax.axis_index("dp")
    me = lax.axis_index("expert")
    width = tokens_ref.shape[1]
    units = wup.shape[1]
    cols = width // groups
    chunks = n // CHUNK
    lead = chunks // 2 * CHUNK
    pairs = (
        (ids_hbm, ids_ref), (tokens_hbm, tokens_ref), (gate_hbm, gate_ref), (cot_hbm, cot_ref),
        (wup_hbm, wup), (wdn_hbm, wdn),
    )
    loads = [pltpu.make_async_copy(src, dst, in_sem.at[i]) for i, (src, dst) in enumerate(pairs)]
    for copy in loads[:4]:
        copy.start()

    barrier = pltpu.get_barrier_semaphore()

    @pl.loop(1, n)
    def _(k):
        pl.semaphore_signal(
            barrier, inc=1, device_id=(dp, lax.rem(me + k, n)), device_id_type=MESH
        )

    @pl.loop(1, groups)
    def _(d):
        pl.semaphore_signal(
            barrier, inc=1, device_id=(lax.rem(dp + d, groups), me), device_id_type=MESH
        )

    loads[0].wait()
    offset, rank, kept = place(ids_ref[...], me, n, capacity)
    t = tokens_ref.shape[0]
    target = jnp.where(kept, offset * pad + rank, -1)
    rows = CHUNK * pad
    step = 512 if width % 512 == 0 else width
    for copy in loads[1:4]:
        copy.wait()
    for copy in loads[4:]:
        copy.start()
    scaled[...] = (column(gate_ref[...]) * cot_ref[...].astype(F32)).astype(BF16)

    def build(c):
        slot = lax.broadcasted_iota(jnp.int32, (rows, t), 0) + c * rows
        select = (slot == target).astype(F32).astype(BF16)
        for at in range(0, width, step):
            x = jnp.dot(select, tokens_ref[:, at : at + step], preferred_element_type=F32)
            y = jnp.dot(select, scaled[:, at : at + step], preferred_element_type=F32)
            both = jnp.concatenate([x.reshape(CHUNK, pad, step), y.reshape(CHUNK, pad, step)], axis=1)
            both = both.astype(BF16)
            send[pl.ds(c * CHUNK, CHUNK), :, at : at + step] = both
            if isinstance(c, int) and c == 0:
                recv[0, :, at : at + step] = both[0]

    build(chunks // 2)
    pl.semaphore_wait(barrier, n - 1 + groups - 1)

    def forth(k):
        return pltpu.make_async_remote_copy(
            src_ref=send.at[k], dst_ref=recv.at[k], send_sem=send_sem.at[k],
            recv_sem=recv_sem.at[k], device_id=(dp, lax.rem(me + k, n)), device_id_type=MESH,
        )

    def home(k):
        return pltpu.make_async_remote_copy(
            src_ref=ret.at[k], dst_ref=back_ref.at[k], send_sem=rsend_sem.at[k],
            recv_sem=rrecv_sem.at[k], device_id=(dp, lax.rem(me + n - k, n)), device_id_type=MESH,
        )

    def a_remote(c, d):
        peer = lax.rem(dp + d, groups)
        return pltpu.make_async_remote_copy(
            src_ref=recv.at[
                pl.ds(c * CHUNK, CHUNK), :, pl.ds(pl.multiple_of(peer * cols, 128), cols)
            ],
            dst_ref=a_all.at[d - 1, pl.ds(c * CHUNK, CHUNK)], send_sem=asend_sem.at[d - 1, c],
            recv_sem=arecv_sem.at[d - 1, c], device_id=(peer, me), device_id_type=MESH,
        )

    def h_remote(c, d):
        peer = lax.rem(dp + d, groups)
        return pltpu.make_async_remote_copy(
            src_ref=hg.at[pl.ds(c * CHUNK, CHUNK)],
            dst_ref=hg_all.at[d - 1, pl.ds(c * CHUNK, CHUNK)], send_sem=hsend_sem.at[d - 1, c],
            recv_sem=hrecv_sem.at[d - 1, c], device_id=(peer, me), device_id_type=MESH,
        )

    for k in range(lead, lead + CHUNK):
        forth(k).start()
    build(0)
    for k in range(1, CHUNK):
        forth(k).start()

    @pl.loop(1, chunks)
    def _(c):
        @pl.when(c != chunks // 2)
        def _():
            build(c)

    slots = n * 2 * pad
    there = column(jnp.where(kept, offset * (2 * pad) + rank, -2 * pad))
    slot = lax.broadcasted_iota(jnp.int32, (t, slots), 1)
    pick[0] = (slot == there).astype(F32).astype(BF16)
    pick[1] = (slot == there + pad).astype(F32).astype(BF16)
    pick_copy = pltpu.make_async_copy(pick, pick_out, out_sem.at[0])
    pick_copy.start()

    for k in range(lead, lead + CHUNK // 2):
        forth(k).wait_send()

    @pl.loop(CHUNK, n)
    def _(k):
        @pl.when((k < lead) | (k >= lead + CHUNK))
        def _():
            forth(k).start()

    for copy in loads[4:]:
        copy.wait()

    nt = (((1,), (1,)), ((), ()))

    @pl.loop(0, chunks)
    def _(i):
        c = jnp.where(i == 0, chunks // 2, jnp.where(i <= chunks // 2, i - 1, i))

        @pl.loop(0, CHUNK)
        def _(j):
            k = c * CHUNK + j

            @pl.when(k > 0)
            def _():
                forth(k).wait_recv()

        @pl.loop(1, groups)
        def _(d):
            a_remote(c, d).start()

        a = recv[pl.ds(c * CHUNK, CHUNK)].reshape(2 * rows, width)
        pre = jnp.dot(a, wup[...], preferred_element_type=F32)
        grad = lax.dot_general(a, wdn[...], nt, preferred_element_type=F32)
        pre = pre.reshape(CHUNK, 2, pad, units)[:, 0]
        grad = grad.reshape(CHUNK, 2, pad, units)[:, 1]
        sigma = 1.0 / (1.0 + jnp.exp(-pre))
        hidden = pre * sigma
        grad = grad * sigma * (1.0 + pre * (1.0 - sigma))
        hg[pl.ds(c * CHUNK, CHUNK)] = jnp.concatenate([grad, hidden], axis=1).astype(BF16)

        @pl.loop(1, groups)
        def _(d):
            h_remote(c, d).start()

        hidden = hidden.reshape(rows, units).astype(BF16)
        grad = grad.reshape(rows, units).astype(BF16)
        for at in range(0, width, step):
            out = jnp.dot(hidden, wdn[:, at : at + step], preferred_element_type=F32)
            tok = lax.dot_general(grad, wup[at : at + step, :], nt, preferred_element_type=F32)
            both = jnp.concatenate(
                [tok.reshape(CHUNK, pad, step), out.reshape(CHUNK, pad, step)], axis=1
            )
            ret[pl.ds(c * CHUNK, CHUNK), :, at : at + step] = both.astype(BF16)

        @pl.loop(0, CHUNK)
        def _(j):
            k = c * CHUNK + j

            @pl.when(k > 0)
            def _():
                home(k).start()

    own = pltpu.make_async_copy(ret.at[0], back_ref.at[0], out_sem.at[1])
    own.start()

    inverse = 1.0 / groups
    tile = 256 if cols % 256 == 0 else cols
    tn = (((0,), (0,)), ((), ()))

    def add_group(a_tile, grads, add):
        grads = grads.reshape(slots, units)
        first = lax.rem(lax.broadcasted_iota(jnp.int32, grads.shape, 0), 2 * pad) < pad
        zero = jnp.zeros_like(grads)
        grad = jnp.where(first, grads, zero)
        hidden = jnp.where(first, zero, grads)
        for at in range(0, cols, tile):
            a = a_tile(at).reshape(slots, tile)
            up = lax.dot_general(a, grad, tn, preferred_element_type=F32) * inverse
            down = lax.dot_general(hidden, a, tn, preferred_element_type=F32) * inverse
            if add:
                up += up_acc[at : at + tile, :]
                down += down_acc[:, at : at + tile]
            up_acc[at : at + tile, :] = up
            down_acc[:, at : at + tile] = down

    add_group(
        lambda at: recv[:, :, pl.ds(pl.multiple_of(dp * cols + at, 128), tile)], hg[...], False
    )

    @pl.loop(1, groups)
    def _(d):
        @pl.loop(0, chunks)
        def _(c):
            a_remote(c, d).wait_recv()
            h_remote(c, d).wait_recv()

        add_group(lambda at: a_all[d - 1, :, :, at : at + tile], hg_all[d - 1], True)

    up_copy = pltpu.make_async_copy(up_acc, up_out, out_sem.at[2])
    down_copy = pltpu.make_async_copy(down_acc, down_out, out_sem.at[3])
    up_copy.start()
    down_copy.start()

    @pl.loop(1, groups)
    def _(d):
        @pl.loop(0, chunks)
        def _(c):
            a_remote(c, d).wait_send()
            h_remote(c, d).wait_send()

    for copy in (pick_copy, own, up_copy, down_copy):
        copy.wait()

    @pl.loop(1, n)
    def _(k):
        @pl.when((k < lead) | (k >= lead + CHUNK // 2))
        def _():
            forth(k).wait_send()

        home(k).wait()


def nbytes(arrays):
    return sum(math.prod(shape) * jnp.dtype(kind).itemsize for shape, kind in arrays)


def exchange(n, groups, capacity, pad, ids, gate, tokens, cot, wup, wdn):
    t, width = tokens.shape
    units = wup.shape[1]
    cols = width // groups
    chunks = n // CHUNK
    hbm = pl.BlockSpec(memory_space=pltpu.HBM)
    anywhere = pl.BlockSpec(memory_space=pl.ANY)
    dma = pltpu.SemaphoreType.DMA
    block = (n, 2 * pad, width)
    buffers = [
        ((1, t), jnp.int32), ((1, t), F32), ((t, width), BF16), ((t, width), BF16),
        ((t, width), BF16), (wup.shape, BF16), (wdn.shape, BF16), (block, BF16), (block, BF16), (block, BF16),
        ((n, 2 * pad, units), BF16),
        ((groups - 1, n, 2 * pad, cols), BF16), ((groups - 1, n, 2 * pad, units), BF16),
        ((cols, units), F32), ((units, cols), F32), ((2, t, n * 2 * pad), BF16),
    ]
    results = [
        (block, BF16), ((cols, units), F32), ((units, cols), F32), ((2, t, n * 2 * pad), BF16),
    ]
    limit = nbytes(buffers) + 10 * 2**20
    near = limit + nbytes(results) < 52 * 2**20
    place_of = pltpu.VMEM if near else jax.ShapeDtypeStruct
    return pl.pallas_call(
        functools.partial(exchange_kernel, n, groups, capacity, pad),
        out_shape=tuple(place_of(shape, kind) for shape, kind in results),
        in_specs=[hbm] * 6,
        out_specs=(anywhere,) * 4,
        scratch_shapes=[pltpu.VMEM(shape, kind) for shape, kind in buffers]
        + [
            dma((6,)), dma((4,)), dma((n,)), dma((n,)), dma((n,)), dma((n,)),
            dma((groups - 1, chunks)), dma((groups - 1, chunks)),
            dma((groups - 1, chunks)), dma((groups - 1, chunks)),
        ],
        compiler_params=pltpu.CompilerParams(
            collective_id=0, has_side_effects=True, vmem_limit_bytes=limit
        ),
        name="expert_exchange",
    )(*(pltpu.with_memory_space_constraint(x, pltpu.HBM) for x in (ids, gate, tokens, cot, wup, wdn)))


def finish_kernel(
    gate_ref, pick_ref, back_ref, up_ref, down_ref, out_ref, tok_ref, up_out, down_out,
    out_buf, tok_buf, sem, row_sem,
):
    parts = sem.shape[1]
    copies = []
    for which, (src, dst) in enumerate(((up_ref, up_out), (down_ref, down_out))):
        size = src.shape[0] // parts
        for i in range(parts):
            rows = pl.ds(i * size, size)
            copies.append(pltpu.make_async_copy(src.at[rows], dst.at[rows], sem.at[which, i]))
    for copy in copies:
        copy.start()
    gate = column(gate_ref[...])
    width = out_ref.shape[1]
    step = 512 if width % 512 == 0 else width
    for i in range(width // step):
        at = pl.ds(i * step, step)
        rows = back_ref[:, at]
        tok = jnp.dot(pick_ref[0], rows, preferred_element_type=F32).astype(BF16)
        tok_buf[:, at] = tok
        out = jnp.dot(pick_ref[1], rows, preferred_element_type=F32)
        out_buf[:, at] = (gate * out).astype(BF16)
        for j, (src, dst) in enumerate(((tok_buf, tok_ref), (out_buf, out_ref))):
            copies.append(
                pltpu.make_async_copy(src.at[:, at], dst.at[:, at], row_sem.at[j, i])
            )
            copies[-1].start()
    for copy in copies:
        copy.wait()


def finish(gate, pick, back, up, down):
    t, width = gate.shape[1], back.shape[1]
    vmem = pl.BlockSpec(memory_space=pltpu.VMEM)
    anywhere = pl.BlockSpec(memory_space=pl.ANY)
    steps = width // 512 if width % 512 == 0 else 1
    return pl.pallas_call(
        finish_kernel,
        out_shape=(
            jax.ShapeDtypeStruct((t, width), BF16),
            jax.ShapeDtypeStruct((t, width), BF16),
            jax.ShapeDtypeStruct(up.shape, F32),
            jax.ShapeDtypeStruct(down.shape, F32),
        ),
        in_specs=[vmem, vmem, vmem, anywhere, anywhere],
        out_specs=(anywhere,) * 4,
        scratch_shapes=[
            pltpu.VMEM((t, width), BF16), pltpu.VMEM((t, width), BF16),
            pltpu.SemaphoreType.DMA((2, 4)), pltpu.SemaphoreType.DMA((2, steps)),
        ],
        compiler_params=pltpu.CompilerParams(vmem_limit_bytes=16 * 2**20),
        name="finish",
    )(gate, pick, back, up, down)


def shards(tokens, expert_ids, gate, cotangent, w_up, w_down):
    t = tokens.shape[0]
    n = lax.axis_size("expert")
    groups = lax.axis_size("dp")
    capacity = t // n
    pad = -(-capacity // 8) * 8
    gate = gate[None]
    back, up, down, pick = exchange(
        n, groups, capacity, pad, expert_ids[None], gate, tokens, cotangent, w_up[0], w_down[0]
    )
    out, tok, up, down = finish(gate, pick, back.reshape(n * 2 * pad, -1), up, down)
    return out, tok, up[None], down[None]


def solution(mesh):
    in_specs = (
        P(("dp", "expert"), None),
        P(("dp", "expert")),
        P(("dp", "expert")),
        P(("dp", "expert"), None),
        P("expert", None, None),
        P("expert", None, None),
    )
    out_specs = (
        P(("dp", "expert"), None),
        P(("dp", "expert"), None),
        P("expert", "dp", None),
        P("expert", None, "dp"),
    )
    return jax.shard_map(shards, mesh=mesh, in_specs=in_specs, out_specs=out_specs, check_vma=False)
```

```python
import functools
import math

import jax
import jax.numpy as jnp
from jax import lax
from jax.experimental import pallas as pl
from jax.experimental.pallas import tpu as pltpu
from jax.sharding import PartitionSpec as P

MESH = pl.DeviceIdType.MESH
F32 = jnp.float32
BF16 = jnp.bfloat16
CHUNK = 4


def column(row):
    t = row.shape[1]
    eye = lax.broadcasted_iota(jnp.int32, (t, t), 0) == lax.broadcasted_iota(jnp.int32, (t, t), 1)
    return jnp.sum(jnp.where(eye, row, jnp.zeros_like(row)), axis=1, keepdims=True)


def partner(me, k, n):
    out, bit = 0, 1
    while bit < n:
        out = out + bit * lax.rem(me // bit + k // bit, 2)
        bit *= 2
    return out


def place(ids, me, n, capacity):
    t = ids.shape[1]
    onehot = lax.broadcasted_iota(jnp.int32, (n, t), 0) == ids
    before = lax.broadcasted_iota(jnp.int32, (t, t), 0) < lax.broadcasted_iota(jnp.int32, (t, t), 1)
    counts = jnp.dot(
        onehot.astype(F32).astype(BF16), before.astype(F32).astype(BF16), preferred_element_type=F32
    )
    rank = jnp.sum(jnp.where(onehot, counts, 0.0), axis=0, keepdims=True).astype(jnp.int32)
    return ids ^ me, rank, rank < capacity


def exchange_kernel(
    n, groups, capacity, pad, ids_hbm, gate_hbm, tokens_hbm, cot_hbm, wup_hbm, wdn_hbm,
    back_ref, up_out, down_out, pick_out,
    ids_ref, gate_ref, tokens_ref, cot_ref, scaled, wup, wdn, send, recv, ret, hg, a_all, hg_all,
    up_acc, down_acc, pick,
    in_sem, out_sem, send_sem, recv_sem, rsend_sem, rrecv_sem,
    asend_sem, arecv_sem, hsend_sem, hrecv_sem,
):
    dp = lax.axis_index("dp")
    me = lax.axis_index("expert")
    width = tokens_ref.shape[1]
    units = wup.shape[1]
    cols = width // groups
    chunks = n // CHUNK
    lead = chunks // 2 * CHUNK
    pairs = (
        (ids_hbm, ids_ref), (tokens_hbm, tokens_ref), (gate_hbm, gate_ref), (cot_hbm, cot_ref),
        (wup_hbm, wup), (wdn_hbm, wdn),
    )
    loads = [pltpu.make_async_copy(src, dst, in_sem.at[i]) for i, (src, dst) in enumerate(pairs)]
    for copy in loads[:4]:
        copy.start()

    barrier = pltpu.get_barrier_semaphore()

    @pl.loop(1, n)
    def _(k):
        pl.semaphore_signal(
            barrier, inc=1, device_id=(dp, partner(me, k, n)), device_id_type=MESH
        )

    @pl.loop(1, groups)
    def _(d):
        pl.semaphore_signal(
            barrier, inc=1, device_id=(lax.rem(dp + d, groups), me), device_id_type=MESH
        )

    loads[0].wait()
    offset, rank, kept = place(ids_ref[...], me, n, capacity)
    t = tokens_ref.shape[0]
    target = jnp.where(kept, offset * pad + rank, -1)
    rows = CHUNK * pad
    step = 512 if width % 512 == 0 else width
    for copy in loads[1:4]:
        copy.wait()
    for copy in loads[4:]:
        copy.start()
    scaled[...] = (column(gate_ref[...]) * cot_ref[...].astype(F32)).astype(BF16)

    def build(c):
        slot = lax.broadcasted_iota(jnp.int32, (rows, t), 0) + c * rows
        select = (slot == target).astype(F32).astype(BF16)
        for at in range(0, width, step):
            x = jnp.dot(select, tokens_ref[:, at : at + step], preferred_element_type=F32)
            y = jnp.dot(select, scaled[:, at : at + step], preferred_element_type=F32)
            both = jnp.concatenate([x.reshape(CHUNK, pad, step), y.reshape(CHUNK, pad, step)], axis=1)
            both = both.astype(BF16)
            send[pl.ds(c * CHUNK, CHUNK), :, at : at + step] = both
            if isinstance(c, int) and c == 0:
                recv[0, :, at : at + step] = both[0]

    build(chunks // 2)
    pl.semaphore_wait(barrier, n - 1 + groups - 1)

    def forth(k):
        return pltpu.make_async_remote_copy(
            src_ref=send.at[k], dst_ref=recv.at[k], send_sem=send_sem.at[k],
            recv_sem=recv_sem.at[k], device_id=(dp, partner(me, k, n)), device_id_type=MESH,
        )

    def home(k):
        return pltpu.make_async_remote_copy(
            src_ref=ret.at[k], dst_ref=back_ref.at[k], send_sem=rsend_sem.at[k],
            recv_sem=rrecv_sem.at[k], device_id=(dp, partner(me, k, n)), device_id_type=MESH,
        )

    def a_remote(c, d):
        peer = lax.rem(dp + d, groups)
        return pltpu.make_async_remote_copy(
            src_ref=recv.at[
                pl.ds(c * CHUNK, CHUNK), :, pl.ds(pl.multiple_of(peer * cols, 128), cols)
            ],
            dst_ref=a_all.at[d - 1, pl.ds(c * CHUNK, CHUNK)], send_sem=asend_sem.at[d - 1, c],
            recv_sem=arecv_sem.at[d - 1, c], device_id=(peer, me), device_id_type=MESH,
        )

    def h_remote(c, d):
        peer = lax.rem(dp + d, groups)
        return pltpu.make_async_remote_copy(
            src_ref=hg.at[pl.ds(c * CHUNK, CHUNK)],
            dst_ref=hg_all.at[d - 1, pl.ds(c * CHUNK, CHUNK)], send_sem=hsend_sem.at[d - 1, c],
            recv_sem=hrecv_sem.at[d - 1, c], device_id=(peer, me), device_id_type=MESH,
        )

    for k in range(lead, lead + CHUNK):
        forth(k).start()
    build(0)
    for k in range(1, CHUNK):
        forth(k).start()

    @pl.loop(1, chunks)
    def _(c):
        @pl.when(c != chunks // 2)
        def _():
            build(c)

    slots = n * 2 * pad
    there = column(jnp.where(kept, offset * (2 * pad) + rank, -2 * pad))
    slot = lax.broadcasted_iota(jnp.int32, (t, slots), 1)
    pick[0] = (slot == there).astype(F32).astype(BF16)
    pick[1] = (slot == there + pad).astype(F32).astype(BF16)
    pick_copy = pltpu.make_async_copy(pick, pick_out, out_sem.at[0])
    pick_copy.start()

    for k in range(lead, lead + CHUNK // 2):
        forth(k).wait_send()

    @pl.loop(0, n - CHUNK)
    def _(i):
        k = n - 1 - i

        @pl.when((k < lead) | (k >= lead + CHUNK))
        def _():
            forth(k).start()

    for copy in loads[4:]:
        copy.wait()

    nt = (((1,), (1,)), ((), ()))

    @pl.loop(0, chunks)
    def _(i):
        c = jnp.where(i == 0, chunks // 2, jnp.where(i <= chunks // 2, i - 1, i))

        @pl.loop(0, CHUNK)
        def _(j):
            k = c * CHUNK + j

            @pl.when(k > 0)
            def _():
                forth(k).wait_recv()

        @pl.loop(1, groups)
        def _(d):
            a_remote(c, d).start()

        a = recv[pl.ds(c * CHUNK, CHUNK)].reshape(2 * rows, width)
        pre = jnp.dot(a, wup[...], preferred_element_type=F32)
        grad = lax.dot_general(a, wdn[...], nt, preferred_element_type=F32)
        pre = pre.reshape(CHUNK, 2, pad, units)[:, 0]
        grad = grad.reshape(CHUNK, 2, pad, units)[:, 1]
        sigma = 1.0 / (1.0 + jnp.exp(-pre))
        hidden = pre * sigma
        grad = grad * sigma * (1.0 + pre * (1.0 - sigma))
        hg[pl.ds(c * CHUNK, CHUNK)] = jnp.concatenate([grad, hidden], axis=1).astype(BF16)

        @pl.loop(1, groups)
        def _(d):
            h_remote(c, d).start()

        hidden = hidden.reshape(rows, units).astype(BF16)
        grad = grad.reshape(rows, units).astype(BF16)
        for at in range(0, width, step):
            out = jnp.dot(hidden, wdn[:, at : at + step], preferred_element_type=F32)
            tok = lax.dot_general(grad, wup[at : at + step, :], nt, preferred_element_type=F32)
            both = jnp.concatenate(
                [tok.reshape(CHUNK, pad, step), out.reshape(CHUNK, pad, step)], axis=1
            )
            ret[pl.ds(c * CHUNK, CHUNK), :, at : at + step] = both.astype(BF16)

        @pl.loop(0, CHUNK)
        def _(j):
            k = c * CHUNK + j

            @pl.when(k > 0)
            def _():
                home(k).start()

    own = pltpu.make_async_copy(ret.at[0], back_ref.at[0], out_sem.at[1])
    own.start()

    inverse = 1.0 / groups
    tile = 256 if cols % 256 == 0 else cols
    tn = (((0,), (0,)), ((), ()))

    def add_group(a_tile, grads, add):
        grads = grads.reshape(slots, units)
        first = lax.rem(lax.broadcasted_iota(jnp.int32, grads.shape, 0), 2 * pad) < pad
        zero = jnp.zeros_like(grads)
        grad = jnp.where(first, grads, zero)
        hidden = jnp.where(first, zero, grads)
        for at in range(0, cols, tile):
            a = a_tile(at).reshape(slots, tile)
            up = lax.dot_general(a, grad, tn, preferred_element_type=F32) * inverse
            down = lax.dot_general(hidden, a, tn, preferred_element_type=F32) * inverse
            if add:
                up += up_acc[at : at + tile, :]
                down += down_acc[:, at : at + tile]
            up_acc[at : at + tile, :] = up
            down_acc[:, at : at + tile] = down

    add_group(
        lambda at: recv[:, :, pl.ds(pl.multiple_of(dp * cols + at, 128), tile)], hg[...], False
    )

    @pl.loop(1, groups)
    def _(d):
        @pl.loop(0, chunks)
        def _(c):
            a_remote(c, d).wait_recv()
            h_remote(c, d).wait_recv()

        add_group(lambda at: a_all[d - 1, :, :, at : at + tile], hg_all[d - 1], True)

    up_copy = pltpu.make_async_copy(up_acc, up_out, out_sem.at[2])
    down_copy = pltpu.make_async_copy(down_acc, down_out, out_sem.at[3])
    up_copy.start()
    down_copy.start()

    @pl.loop(1, groups)
    def _(d):
        @pl.loop(0, chunks)
        def _(c):
            a_remote(c, d).wait_send()
            h_remote(c, d).wait_send()

    for copy in (pick_copy, own, up_copy, down_copy):
        copy.wait()

    @pl.loop(1, n)
    def _(k):
        @pl.when((k < lead) | (k >= lead + CHUNK // 2))
        def _():
            forth(k).wait_send()

        home(k).wait()


def nbytes(arrays):
    return sum(math.prod(shape) * jnp.dtype(kind).itemsize for shape, kind in arrays)


def exchange(n, groups, capacity, pad, ids, gate, tokens, cot, wup, wdn):
    t, width = tokens.shape
    units = wup.shape[1]
    cols = width // groups
    chunks = n // CHUNK
    hbm = pl.BlockSpec(memory_space=pltpu.HBM)
    anywhere = pl.BlockSpec(memory_space=pl.ANY)
    dma = pltpu.SemaphoreType.DMA
    block = (n, 2 * pad, width)
    buffers = [
        ((1, t), jnp.int32), ((1, t), F32), ((t, width), BF16), ((t, width), BF16),
        ((t, width), BF16), (wup.shape, BF16), (wdn.shape, BF16), (block, BF16), (block, BF16), (block, BF16),
        ((n, 2 * pad, units), BF16),
        ((groups - 1, n, 2 * pad, cols), BF16), ((groups - 1, n, 2 * pad, units), BF16),
        ((cols, units), F32), ((units, cols), F32), ((2, t, n * 2 * pad), BF16),
    ]
    results = [
        (block, BF16), ((cols, units), F32), ((units, cols), F32), ((2, t, n * 2 * pad), BF16),
    ]
    limit = nbytes(buffers) + 10 * 2**20
    near = limit + nbytes(results) < 52 * 2**20
    place_of = pltpu.VMEM if near else jax.ShapeDtypeStruct
    return pl.pallas_call(
        functools.partial(exchange_kernel, n, groups, capacity, pad),
        out_shape=tuple(place_of(shape, kind) for shape, kind in results),
        in_specs=[hbm] * 6,
        out_specs=(anywhere,) * 4,
        scratch_shapes=[pltpu.VMEM(shape, kind) for shape, kind in buffers]
        + [
            dma((6,)), dma((4,)), dma((n,)), dma((n,)), dma((n,)), dma((n,)),
            dma((groups - 1, chunks)), dma((groups - 1, chunks)),
            dma((groups - 1, chunks)), dma((groups - 1, chunks)),
        ],
        compiler_params=pltpu.CompilerParams(
            collective_id=0, has_side_effects=True, vmem_limit_bytes=limit
        ),
        name="expert_exchange",
    )(*(pltpu.with_memory_space_constraint(x, pltpu.HBM) for x in (ids, gate, tokens, cot, wup, wdn)))


def finish_kernel(
    gate_ref, pick_ref, back_ref, up_ref, down_ref, out_ref, tok_ref, up_out, down_out,
    out_buf, tok_buf, sem, row_sem,
):
    parts = sem.shape[1]
    copies = []
    for which, (src, dst) in enumerate(((up_ref, up_out), (down_ref, down_out))):
        size = src.shape[0] // parts
        for i in range(parts):
            rows = pl.ds(i * size, size)
            copies.append(pltpu.make_async_copy(src.at[rows], dst.at[rows], sem.at[which, i]))
    for copy in copies:
        copy.start()
    gate = column(gate_ref[...])
    width = out_ref.shape[1]
    step = 512 if width % 512 == 0 else width
    for i in range(width // step):
        at = pl.ds(i * step, step)
        rows = back_ref[:, at]
        tok = jnp.dot(pick_ref[0], rows, preferred_element_type=F32).astype(BF16)
        tok_buf[:, at] = tok
        out = jnp.dot(pick_ref[1], rows, preferred_element_type=F32)
        out_buf[:, at] = (gate * out).astype(BF16)
        for j, (src, dst) in enumerate(((tok_buf, tok_ref), (out_buf, out_ref))):
            copies.append(
                pltpu.make_async_copy(src.at[:, at], dst.at[:, at], row_sem.at[j, i])
            )
            copies[-1].start()
    for copy in copies:
        copy.wait()


def finish(gate, pick, back, up, down):
    t, width = gate.shape[1], back.shape[1]
    vmem = pl.BlockSpec(memory_space=pltpu.VMEM)
    anywhere = pl.BlockSpec(memory_space=pl.ANY)
    steps = width // 512 if width % 512 == 0 else 1
    return pl.pallas_call(
        finish_kernel,
        out_shape=(
            jax.ShapeDtypeStruct((t, width), BF16),
            jax.ShapeDtypeStruct((t, width), BF16),
            jax.ShapeDtypeStruct(up.shape, F32),
            jax.ShapeDtypeStruct(down.shape, F32),
        ),
        in_specs=[vmem, vmem, vmem, anywhere, anywhere],
        out_specs=(anywhere,) * 4,
        scratch_shapes=[
            pltpu.VMEM((t, width), BF16), pltpu.VMEM((t, width), BF16),
            pltpu.SemaphoreType.DMA((2, 4)), pltpu.SemaphoreType.DMA((2, steps)),
        ],
        compiler_params=pltpu.CompilerParams(vmem_limit_bytes=16 * 2**20),
        name="finish",
    )(gate, pick, back, up, down)


def shards(tokens, expert_ids, gate, cotangent, w_up, w_down):
    t = tokens.shape[0]
    n = lax.axis_size("expert")
    groups = lax.axis_size("dp")
    capacity = t // n
    pad = -(-capacity // 8) * 8
    gate = gate[None]
    back, up, down, pick = exchange(
        n, groups, capacity, pad, expert_ids[None], gate, tokens, cotangent, w_up[0], w_down[0]
    )
    out, tok, up, down = finish(gate, pick, back.reshape(n * 2 * pad, -1), up, down)
    return out, tok, up[None], down[None]


def solution(mesh):
    in_specs = (
        P(("dp", "expert"), None),
        P(("dp", "expert")),
        P(("dp", "expert")),
        P(("dp", "expert"), None),
        P("expert", None, None),
        P("expert", None, None),
    )
    out_specs = (
        P(("dp", "expert"), None),
        P(("dp", "expert"), None),
        P("expert", "dp", None),
        P("expert", None, "dp"),
    )
    return jax.shard_map(shards, mesh=mesh, in_specs=in_specs, out_specs=out_specs, check_vma=False)
```

```python
import functools
import math

import jax
import jax.numpy as jnp
from jax import lax
from jax.experimental import pallas as pl
from jax.experimental.pallas import tpu as pltpu
from jax.sharding import PartitionSpec as P

MESH = pl.DeviceIdType.MESH
F32 = jnp.float32
BF16 = jnp.bfloat16
CHUNK = 4


def column(row):
    t = row.shape[1]
    eye = lax.broadcasted_iota(jnp.int32, (t, t), 0) == lax.broadcasted_iota(jnp.int32, (t, t), 1)
    return jnp.sum(jnp.where(eye, row, jnp.zeros_like(row)), axis=1, keepdims=True)


def partner(me, k, n):
    out, bit = 0, 1
    while bit < n:
        out = out + bit * lax.rem(me // bit + k // bit, 2)
        bit *= 2
    return out


def place(ids, me, n, capacity):
    t = ids.shape[1]
    onehot = lax.broadcasted_iota(jnp.int32, (n, t), 0) == ids
    before = lax.broadcasted_iota(jnp.int32, (t, t), 0) < lax.broadcasted_iota(jnp.int32, (t, t), 1)
    counts = jnp.dot(
        onehot.astype(F32).astype(BF16), before.astype(F32).astype(BF16), preferred_element_type=F32
    )
    rank = jnp.sum(jnp.where(onehot, counts, 0.0), axis=0, keepdims=True).astype(jnp.int32)
    return ids ^ me, rank, rank < capacity


def exchange_kernel(
    n, groups, capacity, pad, ids_hbm, gate_hbm, tokens_hbm, cot_hbm, wup_hbm, wdn_hbm,
    back_ref, up_out, down_out, pick_out,
    ids_ref, gate_ref, tokens_ref, cot_ref, scaled, wup, wdn, send, recv, ret, hg, a_all, hg_all,
    up_acc, down_acc, pick,
    in_sem, out_sem, send_sem, recv_sem, rsend_sem, rrecv_sem,
    asend_sem, arecv_sem, hsend_sem, hrecv_sem,
):
    dp = lax.axis_index("dp")
    me = lax.axis_index("expert")
    width = tokens_ref.shape[1]
    units = wup.shape[1]
    cols = width // groups
    chunks = n // CHUNK
    lead = chunks // 2 * CHUNK
    pairs = (
        (ids_hbm, ids_ref), (tokens_hbm, tokens_ref), (gate_hbm, gate_ref), (cot_hbm, cot_ref),
        (wup_hbm, wup), (wdn_hbm, wdn),
    )
    loads = [pltpu.make_async_copy(src, dst, in_sem.at[i]) for i, (src, dst) in enumerate(pairs)]
    for copy in loads[:4]:
        copy.start()

    barrier = pltpu.get_barrier_semaphore()

    @pl.loop(1, n)
    def _(k):
        pl.semaphore_signal(
            barrier, inc=1, device_id=(dp, partner(me, k, n)), device_id_type=MESH
        )

    @pl.loop(1, groups)
    def _(d):
        pl.semaphore_signal(
            barrier, inc=1, device_id=(lax.rem(dp + d, groups), me), device_id_type=MESH
        )

    loads[0].wait()
    offset, rank, kept = place(ids_ref[...], me, n, capacity)
    t = tokens_ref.shape[0]
    target = jnp.where(kept, offset * pad + rank, -1)
    rows = CHUNK * pad
    step = 512 if width % 512 == 0 else width
    for copy in loads[1:4]:
        copy.wait()
    for copy in loads[4:]:
        copy.start()
    scaled[...] = (column(gate_ref[...]) * cot_ref[...].astype(F32)).astype(BF16)

    def build(c):
        slot = lax.broadcasted_iota(jnp.int32, (rows, t), 0) + c * rows
        select = (slot == target).astype(F32).astype(BF16)
        for at in range(0, width, step):
            x = jnp.dot(select, tokens_ref[:, at : at + step], preferred_element_type=F32)
            y = jnp.dot(select, scaled[:, at : at + step], preferred_element_type=F32)
            both = jnp.concatenate([x.reshape(CHUNK, pad, step), y.reshape(CHUNK, pad, step)], axis=1)
            both = both.astype(BF16)
            send[pl.ds(c * CHUNK, CHUNK), :, at : at + step] = both
            if isinstance(c, int) and c == 0:
                recv[0, :, at : at + step] = both[0]

    build(chunks // 2)
    pl.semaphore_wait(barrier, n - 1 + groups - 1)

    def forth(k):
        return pltpu.make_async_remote_copy(
            src_ref=send.at[k], dst_ref=recv.at[k], send_sem=send_sem.at[k],
            recv_sem=recv_sem.at[k], device_id=(dp, partner(me, k, n)), device_id_type=MESH,
        )

    def home(k):
        return pltpu.make_async_remote_copy(
            src_ref=ret.at[k], dst_ref=back_ref.at[k], send_sem=rsend_sem.at[k],
            recv_sem=rrecv_sem.at[k], device_id=(dp, partner(me, k, n)), device_id_type=MESH,
        )

    def a_remote(c, d):
        peer = lax.rem(dp + d, groups)
        return pltpu.make_async_remote_copy(
            src_ref=recv.at[
                pl.ds(c * CHUNK, CHUNK), :, pl.ds(pl.multiple_of(peer * cols, 128), cols)
            ],
            dst_ref=a_all.at[d - 1, pl.ds(c * CHUNK, CHUNK)], send_sem=asend_sem.at[d - 1, c],
            recv_sem=arecv_sem.at[d - 1, c], device_id=(peer, me), device_id_type=MESH,
        )

    def h_remote(c, d):
        peer = lax.rem(dp + d, groups)
        return pltpu.make_async_remote_copy(
            src_ref=hg.at[pl.ds(c * CHUNK, CHUNK)],
            dst_ref=hg_all.at[d - 1, pl.ds(c * CHUNK, CHUNK)], send_sem=hsend_sem.at[d - 1, c],
            recv_sem=hrecv_sem.at[d - 1, c], device_id=(peer, me), device_id_type=MESH,
        )

    for k in range(lead, lead + CHUNK):
        forth(k).start()
    build(0)
    for k in range(1, CHUNK):
        forth(k).start()
    build(1)
    for k in range(CHUNK, 2 * CHUNK):
        forth(k).start()

    @pl.loop(2, chunks)
    def _(c):
        @pl.when(c != chunks // 2)
        def _():
            build(c)

    for copy in loads[4:]:
        copy.wait()

    nt = (((1,), (1,)), ((), ()))

    @pl.loop(0, chunks)
    def _(c):
        @pl.loop(0, CHUNK)
        def _(j):
            k = c * CHUNK + j

            @pl.when(k > 0)
            def _():
                forth(k).wait_recv()

        @pl.loop(1, groups)
        def _(d):
            a_remote(c, d).start()

        a = recv[pl.ds(c * CHUNK, CHUNK)].reshape(2 * rows, width)
        pre = jnp.dot(a, wup[...], preferred_element_type=F32)
        grad = lax.dot_general(a, wdn[...], nt, preferred_element_type=F32)
        pre = pre.reshape(CHUNK, 2, pad, units)[:, 0]
        grad = grad.reshape(CHUNK, 2, pad, units)[:, 1]
        sigma = 1.0 / (1.0 + jnp.exp(-pre))
        hidden = pre * sigma
        grad = grad * sigma * (1.0 + pre * (1.0 - sigma))
        hg[pl.ds(c * CHUNK, CHUNK)] = jnp.concatenate([grad, hidden], axis=1).astype(BF16)

        @pl.loop(1, groups)
        def _(d):
            h_remote(c, d).start()

        hidden = hidden.reshape(rows, units).astype(BF16)
        grad = grad.reshape(rows, units).astype(BF16)
        for at in range(0, width, step):
            out = jnp.dot(hidden, wdn[:, at : at + step], preferred_element_type=F32)
            tok = lax.dot_general(grad, wup[at : at + step, :], nt, preferred_element_type=F32)
            both = jnp.concatenate(
                [tok.reshape(CHUNK, pad, step), out.reshape(CHUNK, pad, step)], axis=1
            )
            ret[pl.ds(c * CHUNK, CHUNK), :, at : at + step] = both.astype(BF16)

        @pl.loop(0, CHUNK)
        def _(j):
            k = c * CHUNK + j

            @pl.when(k > 0)
            def _():
                home(k).start()

        @pl.when(c < 2)
        def _():
            @pl.loop(2, chunks)
            def _(later):
                @pl.when(later != chunks // 2)
                def _():
                    for j in range(CHUNK // 2):
                        forth(later * CHUNK + c * (CHUNK // 2) + j).start()

    slots = n * 2 * pad
    there = column(jnp.where(kept, offset * (2 * pad) + rank, -2 * pad))
    slot = lax.broadcasted_iota(jnp.int32, (t, slots), 1)
    pick[0] = (slot == there).astype(F32).astype(BF16)
    pick[1] = (slot == there + pad).astype(F32).astype(BF16)
    pick_copy = pltpu.make_async_copy(pick, pick_out, out_sem.at[0])
    pick_copy.start()

    own = pltpu.make_async_copy(ret.at[0], back_ref.at[0], out_sem.at[1])
    own.start()

    inverse = 1.0 / groups
    tile = 256 if cols % 256 == 0 else cols
    tn = (((0,), (0,)), ((), ()))

    def add_group(a_tile, grads, add):
        grads = grads.reshape(slots, units)
        first = lax.rem(lax.broadcasted_iota(jnp.int32, grads.shape, 0), 2 * pad) < pad
        zero = jnp.zeros_like(grads)
        grad = jnp.where(first, grads, zero)
        hidden = jnp.where(first, zero, grads)
        for at in range(0, cols, tile):
            a = a_tile(at).reshape(slots, tile)
            up = lax.dot_general(a, grad, tn, preferred_element_type=F32) * inverse
            down = lax.dot_general(hidden, a, tn, preferred_element_type=F32) * inverse
            if add:
                up += up_acc[at : at + tile, :]
                down += down_acc[:, at : at + tile]
            up_acc[at : at + tile, :] = up
            down_acc[:, at : at + tile] = down

    add_group(
        lambda at: recv[:, :, pl.ds(pl.multiple_of(dp * cols + at, 128), tile)], hg[...], False
    )

    @pl.loop(1, groups)
    def _(d):
        @pl.loop(0, chunks)
        def _(c):
            a_remote(c, d).wait_recv()
            h_remote(c, d).wait_recv()

        add_group(lambda at: a_all[d - 1, :, :, at : at + tile], hg_all[d - 1], True)

    up_copy = pltpu.make_async_copy(up_acc, up_out, out_sem.at[2])
    down_copy = pltpu.make_async_copy(down_acc, down_out, out_sem.at[3])
    up_copy.start()
    down_copy.start()

    @pl.loop(1, groups)
    def _(d):
        @pl.loop(0, chunks)
        def _(c):
            a_remote(c, d).wait_send()
            h_remote(c, d).wait_send()

    for copy in (pick_copy, own, up_copy, down_copy):
        copy.wait()

    @pl.loop(1, n)
    def _(k):
        forth(k).wait_send()
        home(k).wait()


def nbytes(arrays):
    return sum(math.prod(shape) * jnp.dtype(kind).itemsize for shape, kind in arrays)


def exchange(n, groups, capacity, pad, ids, gate, tokens, cot, wup, wdn):
    t, width = tokens.shape
    units = wup.shape[1]
    cols = width // groups
    chunks = n // CHUNK
    hbm = pl.BlockSpec(memory_space=pltpu.HBM)
    anywhere = pl.BlockSpec(memory_space=pl.ANY)
    dma = pltpu.SemaphoreType.DMA
    block = (n, 2 * pad, width)
    buffers = [
        ((1, t), jnp.int32), ((1, t), F32), ((t, width), BF16), ((t, width), BF16),
        ((t, width), BF16), (wup.shape, BF16), (wdn.shape, BF16), (block, BF16), (block, BF16), (block, BF16),
        ((n, 2 * pad, units), BF16),
        ((groups - 1, n, 2 * pad, cols), BF16), ((groups - 1, n, 2 * pad, units), BF16),
        ((cols, units), F32), ((units, cols), F32), ((2, t, n * 2 * pad), BF16),
    ]
    results = [
        (block, BF16), ((cols, units), F32), ((units, cols), F32), ((2, t, n * 2 * pad), BF16),
    ]
    limit = nbytes(buffers) + 10 * 2**20
    near = limit + nbytes(results) < 52 * 2**20
    place_of = pltpu.VMEM if near else jax.ShapeDtypeStruct
    return pl.pallas_call(
        functools.partial(exchange_kernel, n, groups, capacity, pad),
        out_shape=tuple(place_of(shape, kind) for shape, kind in results),
        in_specs=[hbm] * 6,
        out_specs=(anywhere,) * 4,
        scratch_shapes=[pltpu.VMEM(shape, kind) for shape, kind in buffers]
        + [
            dma((6,)), dma((4,)), dma((n,)), dma((n,)), dma((n,)), dma((n,)),
            dma((groups - 1, chunks)), dma((groups - 1, chunks)),
            dma((groups - 1, chunks)), dma((groups - 1, chunks)),
        ],
        compiler_params=pltpu.CompilerParams(
            collective_id=0, has_side_effects=True, vmem_limit_bytes=limit
        ),
        name="expert_exchange",
    )(*(pltpu.with_memory_space_constraint(x, pltpu.HBM) for x in (ids, gate, tokens, cot, wup, wdn)))


def finish_kernel(
    gate_ref, pick_ref, back_ref, up_ref, down_ref, out_ref, tok_ref, up_out, down_out,
    out_buf, tok_buf, sem, row_sem,
):
    parts = sem.shape[1]
    copies = []
    for which, (src, dst) in enumerate(((up_ref, up_out), (down_ref, down_out))):
        size = src.shape[0] // parts
        for i in range(parts):
            rows = pl.ds(i * size, size)
            copies.append(pltpu.make_async_copy(src.at[rows], dst.at[rows], sem.at[which, i]))
    for copy in copies:
        copy.start()
    gate = column(gate_ref[...])
    width = out_ref.shape[1]
    step = 512 if width % 512 == 0 else width
    for i in range(width // step):
        at = pl.ds(i * step, step)
        rows = back_ref[:, at]
        tok = jnp.dot(pick_ref[0], rows, preferred_element_type=F32).astype(BF16)
        tok_buf[:, at] = tok
        out = jnp.dot(pick_ref[1], rows, preferred_element_type=F32)
        out_buf[:, at] = (gate * out).astype(BF16)
        for j, (src, dst) in enumerate(((tok_buf, tok_ref), (out_buf, out_ref))):
            copies.append(
                pltpu.make_async_copy(src.at[:, at], dst.at[:, at], row_sem.at[j, i])
            )
            copies[-1].start()
    for copy in copies:
        copy.wait()


def finish(gate, pick, back, up, down):
    t, width = gate.shape[1], back.shape[1]
    vmem = pl.BlockSpec(memory_space=pltpu.VMEM)
    anywhere = pl.BlockSpec(memory_space=pl.ANY)
    steps = width // 512 if width % 512 == 0 else 1
    return pl.pallas_call(
        finish_kernel,
        out_shape=(
            jax.ShapeDtypeStruct((t, width), BF16),
            jax.ShapeDtypeStruct((t, width), BF16),
            jax.ShapeDtypeStruct(up.shape, F32),
            jax.ShapeDtypeStruct(down.shape, F32),
        ),
        in_specs=[vmem, vmem, vmem, anywhere, anywhere],
        out_specs=(anywhere,) * 4,
        scratch_shapes=[
            pltpu.VMEM((t, width), BF16), pltpu.VMEM((t, width), BF16),
            pltpu.SemaphoreType.DMA((2, 4)), pltpu.SemaphoreType.DMA((2, steps)),
        ],
        compiler_params=pltpu.CompilerParams(vmem_limit_bytes=16 * 2**20),
        name="finish",
    )(gate, pick, back, up, down)


def shards(tokens, expert_ids, gate, cotangent, w_up, w_down):
    t = tokens.shape[0]
    n = lax.axis_size("expert")
    groups = lax.axis_size("dp")
    capacity = t // n
    pad = -(-capacity // 8) * 8
    gate = gate[None]
    back, up, down, pick = exchange(
        n, groups, capacity, pad, expert_ids[None], gate, tokens, cotangent, w_up[0], w_down[0]
    )
    out, tok, up, down = finish(gate, pick, back.reshape(n * 2 * pad, -1), up, down)
    return out, tok, up[None], down[None]


def solution(mesh):
    in_specs = (
        P(("dp", "expert"), None),
        P(("dp", "expert")),
        P(("dp", "expert")),
        P(("dp", "expert"), None),
        P("expert", None, None),
        P("expert", None, None),
    )
    out_specs = (
        P(("dp", "expert"), None),
        P(("dp", "expert"), None),
        P("expert", "dp", None),
        P("expert", None, "dp"),
    )
    return jax.shard_map(shards, mesh=mesh, in_specs=in_specs, out_specs=out_specs, check_vma=False)
```

```python
import functools
import math

import jax
import jax.numpy as jnp
from jax import lax
from jax.experimental import pallas as pl
from jax.experimental.pallas import tpu as pltpu
from jax.sharding import PartitionSpec as P

MESH = pl.DeviceIdType.MESH
F32 = jnp.float32
BF16 = jnp.bfloat16
CHUNK = 4


def column(row):
    t = row.shape[1]
    eye = lax.broadcasted_iota(jnp.int32, (t, t), 0) == lax.broadcasted_iota(jnp.int32, (t, t), 1)
    return jnp.sum(jnp.where(eye, row, jnp.zeros_like(row)), axis=1, keepdims=True)


def partner(me, k, n):
    out, bit = 0, 1
    while bit < n:
        out = out + bit * lax.rem(me // bit + k // bit, 2)
        bit *= 2
    return out


def place(ids, me, n, capacity):
    t = ids.shape[1]
    onehot = lax.broadcasted_iota(jnp.int32, (n, t), 0) == ids
    before = lax.broadcasted_iota(jnp.int32, (t, t), 0) < lax.broadcasted_iota(jnp.int32, (t, t), 1)
    counts = jnp.dot(
        onehot.astype(F32).astype(BF16), before.astype(F32).astype(BF16), preferred_element_type=F32
    )
    rank = jnp.sum(jnp.where(onehot, counts, 0.0), axis=0, keepdims=True).astype(jnp.int32)
    return ids ^ me, rank, rank < capacity


def exchange_kernel(
    n, groups, capacity, pad, ids_hbm, gate_hbm, tokens_hbm, cot_hbm, wup_hbm, wdn_hbm,
    back_ref, up_out, down_out, pick_out,
    ids_ref, gate_ref, tokens_ref, cot_ref, scaled, wup, wdn, send, recv, ret, hg, a_all, hg_all,
    up_acc, down_acc, pick,
    in_sem, out_sem, send_sem, recv_sem, rsend_sem, rrecv_sem,
    asend_sem, arecv_sem, hsend_sem, hrecv_sem,
):
    dp = lax.axis_index("dp")
    me = lax.axis_index("expert")
    width = tokens_ref.shape[1]
    units = wup.shape[1]
    cols = width // groups
    chunks = n // CHUNK
    quarter = me // (n // 4)
    middle = (quarter == 1) | (quarter == 2)
    first = jnp.where(middle, chunks - chunks // 4, chunks // 2)
    lead = first * CHUNK
    pairs = (
        (ids_hbm, ids_ref), (tokens_hbm, tokens_ref), (gate_hbm, gate_ref), (cot_hbm, cot_ref),
        (wup_hbm, wup), (wdn_hbm, wdn),
    )
    loads = [pltpu.make_async_copy(src, dst, in_sem.at[i]) for i, (src, dst) in enumerate(pairs)]
    for copy in loads[:4]:
        copy.start()

    barrier = pltpu.get_barrier_semaphore()

    @pl.loop(1, n)
    def _(k):
        pl.semaphore_signal(
            barrier, inc=1, device_id=(dp, partner(me, k, n)), device_id_type=MESH
        )

    @pl.loop(1, groups)
    def _(d):
        pl.semaphore_signal(
            barrier, inc=1, device_id=(lax.rem(dp + d, groups), me), device_id_type=MESH
        )

    loads[0].wait()
    offset, rank, kept = place(ids_ref[...], me, n, capacity)
    t = tokens_ref.shape[0]
    target = jnp.where(kept, offset * pad + rank, -1)
    rows = CHUNK * pad
    step = 512 if width % 512 == 0 else width
    for copy in loads[1:4]:
        copy.wait()
    for copy in loads[4:]:
        copy.start()
    scaled[...] = (column(gate_ref[...]) * cot_ref[...].astype(F32)).astype(BF16)

    def build(c):
        slot = lax.broadcasted_iota(jnp.int32, (rows, t), 0) + c * rows
        select = (slot == target).astype(F32).astype(BF16)
        for at in range(0, width, step):
            x = jnp.dot(select, tokens_ref[:, at : at + step], preferred_element_type=F32)
            y = jnp.dot(select, scaled[:, at : at + step], preferred_element_type=F32)
            both = jnp.concatenate([x.reshape(CHUNK, pad, step), y.reshape(CHUNK, pad, step)], axis=1)
            both = both.astype(BF16)
            send[pl.ds(c * CHUNK, CHUNK), :, at : at + step] = both
            if isinstance(c, int) and c == 0:
                recv[0, :, at : at + step] = both[0]

    build(first)
    pl.semaphore_wait(barrier, n - 1 + groups - 1)

    def forth(k):
        return pltpu.make_async_remote_copy(
            src_ref=send.at[k], dst_ref=recv.at[k], send_sem=send_sem.at[k],
            recv_sem=recv_sem.at[k], device_id=(dp, partner(me, k, n)), device_id_type=MESH,
        )

    def home(k):
        return pltpu.make_async_remote_copy(
            src_ref=ret.at[k], dst_ref=back_ref.at[k], send_sem=rsend_sem.at[k],
            recv_sem=rrecv_sem.at[k], device_id=(dp, partner(me, k, n)), device_id_type=MESH,
        )

    def a_remote(c, d):
        peer = lax.rem(dp + d, groups)
        return pltpu.make_async_remote_copy(
            src_ref=recv.at[
                pl.ds(c * CHUNK, CHUNK), :, pl.ds(pl.multiple_of(peer * cols, 128), cols)
            ],
            dst_ref=a_all.at[d - 1, pl.ds(c * CHUNK, CHUNK)], send_sem=asend_sem.at[d - 1, c],
            recv_sem=arecv_sem.at[d - 1, c], device_id=(peer, me), device_id_type=MESH,
        )

    def h_remote(c, d):
        peer = lax.rem(dp + d, groups)
        return pltpu.make_async_remote_copy(
            src_ref=hg.at[pl.ds(c * CHUNK, CHUNK)],
            dst_ref=hg_all.at[d - 1, pl.ds(c * CHUNK, CHUNK)], send_sem=hsend_sem.at[d - 1, c],
            recv_sem=hrecv_sem.at[d - 1, c], device_id=(peer, me), device_id_type=MESH,
        )

    for j in range(CHUNK):
        forth(lead + j).start()
    build(0)
    for k in range(1, CHUNK):
        forth(k).start()
    build(1)
    for k in range(CHUNK, 2 * CHUNK):
        forth(k).start()

    @pl.loop(2, chunks)
    def _(c):
        @pl.when(c != first)
        def _():
            build(c)

    slots = n * 2 * pad
    there = column(jnp.where(kept, offset * (2 * pad) + rank, -2 * pad))
    slot = lax.broadcasted_iota(jnp.int32, (t, slots), 1)
    pick[0] = (slot == there).astype(F32).astype(BF16)
    pick[1] = (slot == there + pad).astype(F32).astype(BF16)
    pick_copy = pltpu.make_async_copy(pick, pick_out, out_sem.at[0])
    pick_copy.start()

    for j in range(CHUNK // 2):
        forth(lead + j).wait_send()

    @pl.loop(0, n - 2 * CHUNK)
    def _(i):
        k = n - 1 - i

        @pl.when((k < lead) | (k >= lead + CHUNK))
        def _():
            forth(k).start()

    for copy in loads[4:]:
        copy.wait()

    nt = (((1,), (1,)), ((), ()))

    @pl.loop(0, chunks)
    def _(i):
        half = chunks // 2
        ends = jnp.where(i < half, i, chunks - 1 - (i - half))
        c = jnp.where(middle, lax.rem(i + half, chunks), ends)

        @pl.loop(0, CHUNK)
        def _(j):
            k = c * CHUNK + j

            @pl.when(k > 0)
            def _():
                forth(k).wait_recv()

        @pl.loop(1, groups)
        def _(d):
            a_remote(c, d).start()

        a = recv[pl.ds(c * CHUNK, CHUNK)].reshape(2 * rows, width)
        pre = jnp.dot(a, wup[...], preferred_element_type=F32)
        grad = lax.dot_general(a, wdn[...], nt, preferred_element_type=F32)
        pre = pre.reshape(CHUNK, 2, pad, units)[:, 0]
        grad = grad.reshape(CHUNK, 2, pad, units)[:, 1]
        sigma = 1.0 / (1.0 + jnp.exp(-pre))
        hidden = pre * sigma
        grad = grad * sigma * (1.0 + pre * (1.0 - sigma))
        hg[pl.ds(c * CHUNK, CHUNK)] = jnp.concatenate([grad, hidden], axis=1).astype(BF16)

        @pl.loop(1, groups)
        def _(d):
            h_remote(c, d).start()

        hidden = hidden.reshape(rows, units).astype(BF16)
        grad = grad.reshape(rows, units).astype(BF16)
        for at in range(0, width, step):
            out = jnp.dot(hidden, wdn[:, at : at + step], preferred_element_type=F32)
            tok = lax.dot_general(grad, wup[at : at + step, :], nt, preferred_element_type=F32)
            both = jnp.concatenate(
                [tok.reshape(CHUNK, pad, step), out.reshape(CHUNK, pad, step)], axis=1
            )
            ret[pl.ds(c * CHUNK, CHUNK), :, at : at + step] = both.astype(BF16)

        @pl.loop(0, CHUNK)
        def _(j):
            k = c * CHUNK + j

            @pl.when(k > 0)
            def _():
                home(k).start()

    own = pltpu.make_async_copy(ret.at[0], back_ref.at[0], out_sem.at[1])
    own.start()

    inverse = 1.0 / groups
    tile = 256 if cols % 256 == 0 else cols
    tn = (((0,), (0,)), ((), ()))

    def add_group(a_tile, grads, add):
        grads = grads.reshape(slots, units)
        first = lax.rem(lax.broadcasted_iota(jnp.int32, grads.shape, 0), 2 * pad) < pad
        zero = jnp.zeros_like(grads)
        grad = jnp.where(first, grads, zero)
        hidden = jnp.where(first, zero, grads)
        for at in range(0, cols, tile):
            a = a_tile(at).reshape(slots, tile)
            up = lax.dot_general(a, grad, tn, preferred_element_type=F32) * inverse
            down = lax.dot_general(hidden, a, tn, preferred_element_type=F32) * inverse
            if add:
                up += up_acc[at : at + tile, :]
                down += down_acc[:, at : at + tile]
            up_acc[at : at + tile, :] = up
            down_acc[:, at : at + tile] = down

    add_group(
        lambda at: recv[:, :, pl.ds(pl.multiple_of(dp * cols + at, 128), tile)], hg[...], False
    )

    @pl.loop(1, groups)
    def _(d):
        @pl.loop(0, chunks)
        def _(c):
            a_remote(c, d).wait_recv()
            h_remote(c, d).wait_recv()

        add_group(lambda at: a_all[d - 1, :, :, at : at + tile], hg_all[d - 1], True)

    up_copy = pltpu.make_async_copy(up_acc, up_out, out_sem.at[2])
    down_copy = pltpu.make_async_copy(down_acc, down_out, out_sem.at[3])
    up_copy.start()
    down_copy.start()

    @pl.loop(1, groups)
    def _(d):
        @pl.loop(0, chunks)
        def _(c):
            a_remote(c, d).wait_send()
            h_remote(c, d).wait_send()

    for copy in (pick_copy, own, up_copy, down_copy):
        copy.wait()

    @pl.loop(1, n)
    def _(k):
        @pl.when((k < lead) | (k >= lead + CHUNK // 2))
        def _():
            forth(k).wait_send()

        home(k).wait()


def nbytes(arrays):
    return sum(math.prod(shape) * jnp.dtype(kind).itemsize for shape, kind in arrays)


def exchange(n, groups, capacity, pad, ids, gate, tokens, cot, wup, wdn):
    t, width = tokens.shape
    units = wup.shape[1]
    cols = width // groups
    chunks = n // CHUNK
    hbm = pl.BlockSpec(memory_space=pltpu.HBM)
    anywhere = pl.BlockSpec(memory_space=pl.ANY)
    dma = pltpu.SemaphoreType.DMA
    block = (n, 2 * pad, width)
    buffers = [
        ((1, t), jnp.int32), ((1, t), F32), ((t, width), BF16), ((t, width), BF16),
        ((t, width), BF16), (wup.shape, BF16), (wdn.shape, BF16), (block, BF16), (block, BF16), (block, BF16),
        ((n, 2 * pad, units), BF16),
        ((groups - 1, n, 2 * pad, cols), BF16), ((groups - 1, n, 2 * pad, units), BF16),
        ((cols, units), F32), ((units, cols), F32), ((2, t, n * 2 * pad), BF16),
    ]
    results = [
        (block, BF16), ((cols, units), F32), ((units, cols), F32), ((2, t, n * 2 * pad), BF16),
    ]
    limit = nbytes(buffers) + 10 * 2**20
    near = limit + nbytes(results) < 52 * 2**20
    place_of = pltpu.VMEM if near else jax.ShapeDtypeStruct
    return pl.pallas_call(
        functools.partial(exchange_kernel, n, groups, capacity, pad),
        out_shape=tuple(place_of(shape, kind) for shape, kind in results),
        in_specs=[hbm] * 6,
        out_specs=(anywhere,) * 4,
        scratch_shapes=[pltpu.VMEM(shape, kind) for shape, kind in buffers]
        + [
            dma((6,)), dma((4,)), dma((n,)), dma((n,)), dma((n,)), dma((n,)),
            dma((groups - 1, chunks)), dma((groups - 1, chunks)),
            dma((groups - 1, chunks)), dma((groups - 1, chunks)),
        ],
        compiler_params=pltpu.CompilerParams(
            collective_id=0, has_side_effects=True, vmem_limit_bytes=limit
        ),
        name="expert_exchange",
    )(*(pltpu.with_memory_space_constraint(x, pltpu.HBM) for x in (ids, gate, tokens, cot, wup, wdn)))


def finish_kernel(
    gate_ref, pick_ref, back_ref, up_ref, down_ref, out_ref, tok_ref, up_out, down_out,
    out_buf, tok_buf, sem, row_sem,
):
    parts = sem.shape[1]
    copies = []
    for which, (src, dst) in enumerate(((up_ref, up_out), (down_ref, down_out))):
        size = src.shape[0] // parts
        for i in range(parts):
            rows = pl.ds(i * size, size)
            copies.append(pltpu.make_async_copy(src.at[rows], dst.at[rows], sem.at[which, i]))
    for copy in copies:
        copy.start()
    gate = column(gate_ref[...])
    width = out_ref.shape[1]
    step = 512 if width % 512 == 0 else width
    for i in range(width // step):
        at = pl.ds(i * step, step)
        rows = back_ref[:, at]
        tok = jnp.dot(pick_ref[0], rows, preferred_element_type=F32).astype(BF16)
        tok_buf[:, at] = tok
        out = jnp.dot(pick_ref[1], rows, preferred_element_type=F32)
        out_buf[:, at] = (gate * out).astype(BF16)
        for j, (src, dst) in enumerate(((tok_buf, tok_ref), (out_buf, out_ref))):
            copies.append(
                pltpu.make_async_copy(src.at[:, at], dst.at[:, at], row_sem.at[j, i])
            )
            copies[-1].start()
    for copy in copies:
        copy.wait()


def finish(gate, pick, back, up, down):
    t, width = gate.shape[1], back.shape[1]
    vmem = pl.BlockSpec(memory_space=pltpu.VMEM)
    anywhere = pl.BlockSpec(memory_space=pl.ANY)
    steps = width // 512 if width % 512 == 0 else 1
    return pl.pallas_call(
        finish_kernel,
        out_shape=(
            jax.ShapeDtypeStruct((t, width), BF16),
            jax.ShapeDtypeStruct((t, width), BF16),
            jax.ShapeDtypeStruct(up.shape, F32),
            jax.ShapeDtypeStruct(down.shape, F32),
        ),
        in_specs=[vmem, vmem, vmem, anywhere, anywhere],
        out_specs=(anywhere,) * 4,
        scratch_shapes=[
            pltpu.VMEM((t, width), BF16), pltpu.VMEM((t, width), BF16),
            pltpu.SemaphoreType.DMA((2, 4)), pltpu.SemaphoreType.DMA((2, steps)),
        ],
        compiler_params=pltpu.CompilerParams(vmem_limit_bytes=16 * 2**20),
        name="finish",
    )(gate, pick, back, up, down)


def shards(tokens, expert_ids, gate, cotangent, w_up, w_down):
    t = tokens.shape[0]
    n = lax.axis_size("expert")
    groups = lax.axis_size("dp")
    capacity = t // n
    pad = -(-capacity // 8) * 8
    gate = gate[None]
    back, up, down, pick = exchange(
        n, groups, capacity, pad, expert_ids[None], gate, tokens, cotangent, w_up[0], w_down[0]
    )
    out, tok, up, down = finish(gate, pick, back.reshape(n * 2 * pad, -1), up, down)
    return out, tok, up[None], down[None]


def solution(mesh):
    in_specs = (
        P(("dp", "expert"), None),
        P(("dp", "expert")),
        P(("dp", "expert")),
        P(("dp", "expert"), None),
        P("expert", None, None),
        P("expert", None, None),
    )
    out_specs = (
        P(("dp", "expert"), None),
        P(("dp", "expert"), None),
        P("expert", "dp", None),
        P("expert", None, "dp"),
    )
    return jax.shard_map(shards, mesh=mesh, in_specs=in_specs, out_specs=out_specs, check_vma=False)
```

```python
import functools
import math

import jax
import jax.numpy as jnp
from jax import lax
from jax.experimental import pallas as pl
from jax.experimental.pallas import tpu as pltpu
from jax.sharding import PartitionSpec as P

MESH = pl.DeviceIdType.MESH
F32 = jnp.float32
BF16 = jnp.bfloat16
CHUNK = 4


def column(row):
    t = row.shape[1]
    eye = lax.broadcasted_iota(jnp.int32, (t, t), 0) == lax.broadcasted_iota(jnp.int32, (t, t), 1)
    return jnp.sum(jnp.where(eye, row, jnp.zeros_like(row)), axis=1, keepdims=True)


def partner(me, k, n):
    out, bit = 0, 1
    while bit < n:
        out = out + bit * lax.rem(me // bit + k // bit, 2)
        bit *= 2
    return out


def place(ids, me, n, capacity):
    t = ids.shape[1]
    onehot = lax.broadcasted_iota(jnp.int32, (n, t), 0) == ids
    before = lax.broadcasted_iota(jnp.int32, (t, t), 0) < lax.broadcasted_iota(jnp.int32, (t, t), 1)
    counts = jnp.dot(
        onehot.astype(F32).astype(BF16), before.astype(F32).astype(BF16), preferred_element_type=F32
    )
    rank = jnp.sum(jnp.where(onehot, counts, 0.0), axis=0, keepdims=True).astype(jnp.int32)
    return ids ^ me, rank, rank < capacity


def exchange_kernel(
    n, groups, capacity, pad, ids_hbm, gate_hbm, tokens_hbm, cot_hbm, wup_hbm, wdn_hbm,
    back_ref, up_out, down_out, pick_out,
    ids_ref, gate_ref, tokens_ref, cot_ref, scaled, wup, wdn, send, recv, ret, hg, a_all, hg_all,
    up_acc, down_acc, pick,
    in_sem, out_sem, send_sem, recv_sem, rsend_sem, rrecv_sem,
    asend_sem, arecv_sem, hsend_sem, hrecv_sem,
):
    dp = lax.axis_index("dp")
    me = lax.axis_index("expert")
    width = tokens_ref.shape[1]
    units = wup.shape[1]
    cols = width // groups
    chunks = n // CHUNK
    lead = chunks // 2 * CHUNK
    pairs = (
        (ids_hbm, ids_ref), (tokens_hbm, tokens_ref), (gate_hbm, gate_ref), (cot_hbm, cot_ref),
        (wup_hbm, wup), (wdn_hbm, wdn),
    )
    loads = [pltpu.make_async_copy(src, dst, in_sem.at[i]) for i, (src, dst) in enumerate(pairs)]
    for copy in loads[:4]:
        copy.start()

    barrier = pltpu.get_barrier_semaphore()

    @pl.loop(1, n)
    def _(k):
        pl.semaphore_signal(
            barrier, inc=1, device_id=(dp, partner(me, k, n)), device_id_type=MESH
        )

    @pl.loop(1, groups)
    def _(d):
        pl.semaphore_signal(
            barrier, inc=1, device_id=(lax.rem(dp + d, groups), me), device_id_type=MESH
        )

    loads[0].wait()
    offset, rank, kept = place(ids_ref[...], me, n, capacity)
    t = tokens_ref.shape[0]
    target = jnp.where(kept, offset * pad + rank, -1)
    rows = CHUNK * pad
    step = 512 if width % 512 == 0 else width
    for copy in loads[1:4]:
        copy.wait()
    for copy in loads[4:]:
        copy.start()
    scaled[...] = (column(gate_ref[...]) * cot_ref[...].astype(F32)).astype(BF16)

    def build(c):
        slot = lax.broadcasted_iota(jnp.int32, (rows, t), 0) + c * rows
        select = (slot == target).astype(F32).astype(BF16)
        for at in range(0, width, step):
            x = jnp.dot(select, tokens_ref[:, at : at + step], preferred_element_type=F32)
            y = jnp.dot(select, scaled[:, at : at + step], preferred_element_type=F32)
            both = jnp.concatenate([x.reshape(CHUNK, pad, step), y.reshape(CHUNK, pad, step)], axis=1)
            both = both.astype(BF16)
            send[pl.ds(c * CHUNK, CHUNK), :, at : at + step] = both
            if isinstance(c, int) and c == 0:
                recv[0, :, at : at + step] = both[0]

    build(chunks // 2)
    pl.semaphore_wait(barrier, n - 1 + groups - 1)

    def forth(k):
        return pltpu.make_async_remote_copy(
            src_ref=send.at[k], dst_ref=recv.at[k], send_sem=send_sem.at[k],
            recv_sem=recv_sem.at[k], device_id=(dp, partner(me, k, n)), device_id_type=MESH,
        )

    def home(k):
        return pltpu.make_async_remote_copy(
            src_ref=ret.at[k], dst_ref=back_ref.at[k], send_sem=rsend_sem.at[k],
            recv_sem=rrecv_sem.at[k], device_id=(dp, partner(me, k, n)), device_id_type=MESH,
        )

    def a_remote(c, d):
        peer = lax.rem(dp + d, groups)
        return pltpu.make_async_remote_copy(
            src_ref=recv.at[
                pl.ds(c * CHUNK, CHUNK), :, pl.ds(pl.multiple_of(peer * cols, 128), cols)
            ],
            dst_ref=a_all.at[d - 1, pl.ds(c * CHUNK, CHUNK)], send_sem=asend_sem.at[d - 1, c],
            recv_sem=arecv_sem.at[d - 1, c], device_id=(peer, me), device_id_type=MESH,
        )

    def h_remote(c, d):
        peer = lax.rem(dp + d, groups)
        return pltpu.make_async_remote_copy(
            src_ref=hg.at[pl.ds(c * CHUNK, CHUNK)],
            dst_ref=hg_all.at[d - 1, pl.ds(c * CHUNK, CHUNK)], send_sem=hsend_sem.at[d - 1, c],
            recv_sem=hrecv_sem.at[d - 1, c], device_id=(peer, me), device_id_type=MESH,
        )

    for k in range(lead, lead + CHUNK):
        forth(k).start()
    build(0)
    for k in range(1, CHUNK):
        forth(k).start()

    @pl.loop(1, chunks)
    def _(c):
        @pl.when(c != chunks // 2)
        def _():
            build(c)

    for k in range(lead, lead + CHUNK // 2):
        forth(k).wait_send()

    @pl.loop(0, n - CHUNK)
    def _(i):
        k = n - 1 - i

        @pl.when((k < lead) | (k >= lead + CHUNK))
        def _():
            forth(k).start()

    for copy in loads[4:]:
        copy.wait()

    nt = (((1,), (1,)), ((), ()))

    def serve(c, m):
        count = m * CHUNK
        held = pl.ds(c * CHUNK, count)

        @pl.loop(0, count)
        def _(j):
            k = c * CHUNK + j

            @pl.when(k > 0)
            def _():
                forth(k).wait_recv()

        @pl.loop(1, groups)
        def _(d):
            for i in range(m):
                a_remote(c + i, d).start()

        a = recv[held].reshape(m * 2 * rows, width)
        pre = jnp.dot(a, wup[...], preferred_element_type=F32)
        grad = lax.dot_general(a, wdn[...], nt, preferred_element_type=F32)
        pre = pre.reshape(count, 2, pad, units)[:, 0]
        grad = grad.reshape(count, 2, pad, units)[:, 1]
        sigma = 1.0 / (1.0 + jnp.exp(-pre))
        hidden = pre * sigma
        grad = grad * sigma * (1.0 + pre * (1.0 - sigma))
        hg[held] = jnp.concatenate([grad, hidden], axis=1).astype(BF16)

        @pl.loop(1, groups)
        def _(d):
            for i in range(m):
                h_remote(c + i, d).start()

        hidden = hidden.reshape(m * rows, units).astype(BF16)
        grad = grad.reshape(m * rows, units).astype(BF16)
        for at in range(0, width, step):
            out = jnp.dot(hidden, wdn[:, at : at + step], preferred_element_type=F32)
            tok = lax.dot_general(grad, wup[at : at + step, :], nt, preferred_element_type=F32)
            both = jnp.concatenate(
                [tok.reshape(count, pad, step), out.reshape(count, pad, step)], axis=1
            )
            ret[held, :, at : at + step] = both.astype(BF16)

        @pl.loop(0, count)
        def _(j):
            k = c * CHUNK + j

            @pl.when(k > 0)
            def _():
                home(k).start()

    serve(chunks // 2, 1)
    serve(0, 2)

    @pl.loop(2, chunks)
    def _(c):
        @pl.when(c != chunks // 2)
        def _():
            serve(c, 1)

    slots = n * 2 * pad
    there = column(jnp.where(kept, offset * (2 * pad) + rank, -2 * pad))
    slot = lax.broadcasted_iota(jnp.int32, (t, slots), 1)
    pick[0] = (slot == there).astype(F32).astype(BF16)
    pick[1] = (slot == there + pad).astype(F32).astype(BF16)
    pick_copy = pltpu.make_async_copy(pick, pick_out, out_sem.at[0])
    pick_copy.start()

    own = pltpu.make_async_copy(ret.at[0], back_ref.at[0], out_sem.at[1])
    own.start()

    inverse = 1.0 / groups
    tile = 256 if cols % 256 == 0 else cols
    tn = (((0,), (0,)), ((), ()))

    def add_group(a_tile, grads, add):
        grads = grads.reshape(slots, units)
        first = lax.rem(lax.broadcasted_iota(jnp.int32, grads.shape, 0), 2 * pad) < pad
        zero = jnp.zeros_like(grads)
        grad = jnp.where(first, grads, zero)
        hidden = jnp.where(first, zero, grads)
        for at in range(0, cols, tile):
            a = a_tile(at).reshape(slots, tile)
            up = lax.dot_general(a, grad, tn, preferred_element_type=F32) * inverse
            down = lax.dot_general(hidden, a, tn, preferred_element_type=F32) * inverse
            if add:
                up += up_acc[at : at + tile, :]
                down += down_acc[:, at : at + tile]
            up_acc[at : at + tile, :] = up
            down_acc[:, at : at + tile] = down

    add_group(
        lambda at: recv[:, :, pl.ds(pl.multiple_of(dp * cols + at, 128), tile)], hg[...], False
    )

    @pl.loop(1, groups)
    def _(d):
        @pl.loop(0, chunks)
        def _(c):
            a_remote(c, d).wait_recv()
            h_remote(c, d).wait_recv()

        add_group(lambda at: a_all[d - 1, :, :, at : at + tile], hg_all[d - 1], True)

    up_copy = pltpu.make_async_copy(up_acc, up_out, out_sem.at[2])
    down_copy = pltpu.make_async_copy(down_acc, down_out, out_sem.at[3])
    up_copy.start()
    down_copy.start()

    @pl.loop(1, groups)
    def _(d):
        @pl.loop(0, chunks)
        def _(c):
            a_remote(c, d).wait_send()
            h_remote(c, d).wait_send()

    for copy in (pick_copy, own, up_copy, down_copy):
        copy.wait()

    @pl.loop(1, n)
    def _(k):
        @pl.when((k < lead) | (k >= lead + CHUNK // 2))
        def _():
            forth(k).wait_send()

        home(k).wait()


def nbytes(arrays):
    return sum(math.prod(shape) * jnp.dtype(kind).itemsize for shape, kind in arrays)


def exchange(n, groups, capacity, pad, ids, gate, tokens, cot, wup, wdn):
    t, width = tokens.shape
    units = wup.shape[1]
    cols = width // groups
    chunks = n // CHUNK
    hbm = pl.BlockSpec(memory_space=pltpu.HBM)
    anywhere = pl.BlockSpec(memory_space=pl.ANY)
    dma = pltpu.SemaphoreType.DMA
    block = (n, 2 * pad, width)
    buffers = [
        ((1, t), jnp.int32), ((1, t), F32), ((t, width), BF16), ((t, width), BF16),
        ((t, width), BF16), (wup.shape, BF16), (wdn.shape, BF16), (block, BF16), (block, BF16), (block, BF16),
        ((n, 2 * pad, units), BF16),
        ((groups - 1, n, 2 * pad, cols), BF16), ((groups - 1, n, 2 * pad, units), BF16),
        ((cols, units), F32), ((units, cols), F32), ((2, t, n * 2 * pad), BF16),
    ]
    results = [
        (block, BF16), ((cols, units), F32), ((units, cols), F32), ((2, t, n * 2 * pad), BF16),
    ]
    limit = nbytes(buffers) + 10 * 2**20
    near = limit + nbytes(results) < 52 * 2**20
    place_of = pltpu.VMEM if near else jax.ShapeDtypeStruct
    return pl.pallas_call(
        functools.partial(exchange_kernel, n, groups, capacity, pad),
        out_shape=tuple(place_of(shape, kind) for shape, kind in results),
        in_specs=[hbm] * 6,
        out_specs=(anywhere,) * 4,
        scratch_shapes=[pltpu.VMEM(shape, kind) for shape, kind in buffers]
        + [
            dma((6,)), dma((4,)), dma((n,)), dma((n,)), dma((n,)), dma((n,)),
            dma((groups - 1, chunks)), dma((groups - 1, chunks)),
            dma((groups - 1, chunks)), dma((groups - 1, chunks)),
        ],
        compiler_params=pltpu.CompilerParams(
            collective_id=0, has_side_effects=True, vmem_limit_bytes=limit
        ),
        name="expert_exchange",
    )(*(pltpu.with_memory_space_constraint(x, pltpu.HBM) for x in (ids, gate, tokens, cot, wup, wdn)))


def finish_kernel(
    gate_ref, pick_ref, back_ref, up_ref, down_ref, out_ref, tok_ref, up_out, down_out,
    out_buf, tok_buf, sem, row_sem,
):
    parts = sem.shape[1]
    copies = []
    for which, (src, dst) in enumerate(((up_ref, up_out), (down_ref, down_out))):
        size = src.shape[0] // parts
        for i in range(parts):
            rows = pl.ds(i * size, size)
            copies.append(pltpu.make_async_copy(src.at[rows], dst.at[rows], sem.at[which, i]))
    for copy in copies:
        copy.start()
    gate = column(gate_ref[...])
    width = out_ref.shape[1]
    step = 512 if width % 512 == 0 else width
    for i in range(width // step):
        at = pl.ds(i * step, step)
        rows = back_ref[:, at]
        tok = jnp.dot(pick_ref[0], rows, preferred_element_type=F32).astype(BF16)
        tok_buf[:, at] = tok
        out = jnp.dot(pick_ref[1], rows, preferred_element_type=F32)
        out_buf[:, at] = (gate * out).astype(BF16)
        for j, (src, dst) in enumerate(((tok_buf, tok_ref), (out_buf, out_ref))):
            copies.append(
                pltpu.make_async_copy(src.at[:, at], dst.at[:, at], row_sem.at[j, i])
            )
            copies[-1].start()
    for copy in copies:
        copy.wait()


def finish(gate, pick, back, up, down):
    t, width = gate.shape[1], back.shape[1]
    vmem = pl.BlockSpec(memory_space=pltpu.VMEM)
    anywhere = pl.BlockSpec(memory_space=pl.ANY)
    steps = width // 512 if width % 512 == 0 else 1
    return pl.pallas_call(
        finish_kernel,
        out_shape=(
            jax.ShapeDtypeStruct((t, width), BF16),
            jax.ShapeDtypeStruct((t, width), BF16),
            jax.ShapeDtypeStruct(up.shape, F32),
            jax.ShapeDtypeStruct(down.shape, F32),
        ),
        in_specs=[vmem, vmem, vmem, anywhere, anywhere],
        out_specs=(anywhere,) * 4,
        scratch_shapes=[
            pltpu.VMEM((t, width), BF16), pltpu.VMEM((t, width), BF16),
            pltpu.SemaphoreType.DMA((2, 4)), pltpu.SemaphoreType.DMA((2, steps)),
        ],
        compiler_params=pltpu.CompilerParams(vmem_limit_bytes=16 * 2**20),
        name="finish",
    )(gate, pick, back, up, down)


def shards(tokens, expert_ids, gate, cotangent, w_up, w_down):
    t = tokens.shape[0]
    n = lax.axis_size("expert")
    groups = lax.axis_size("dp")
    capacity = t // n
    pad = -(-capacity // 8) * 8
    gate = gate[None]
    back, up, down, pick = exchange(
        n, groups, capacity, pad, expert_ids[None], gate, tokens, cotangent, w_up[0], w_down[0]
    )
    out, tok, up, down = finish(gate, pick, back.reshape(n * 2 * pad, -1), up, down)
    return out, tok, up[None], down[None]


def solution(mesh):
    in_specs = (
        P(("dp", "expert"), None),
        P(("dp", "expert")),
        P(("dp", "expert")),
        P(("dp", "expert"), None),
        P("expert", None, None),
        P("expert", None, None),
    )
    out_specs = (
        P(("dp", "expert"), None),
        P(("dp", "expert"), None),
        P("expert", "dp", None),
        P("expert", None, "dp"),
    )
    return jax.shard_map(shards, mesh=mesh, in_specs=in_specs, out_specs=out_specs, check_vma=False)
```

```python
import functools
import math

import jax
import jax.numpy as jnp
from jax import lax
from jax.experimental import pallas as pl
from jax.experimental.pallas import tpu as pltpu
from jax.sharding import PartitionSpec as P

MESH = pl.DeviceIdType.MESH
F32 = jnp.float32
BF16 = jnp.bfloat16
CHUNK = 4


def column(row):
    t = row.shape[1]
    eye = lax.broadcasted_iota(jnp.int32, (t, t), 0) == lax.broadcasted_iota(jnp.int32, (t, t), 1)
    return jnp.sum(jnp.where(eye, row, jnp.zeros_like(row)), axis=1, keepdims=True)


def partner(me, k, n):
    out, bit = 0, 1
    while bit < n:
        out = out + bit * lax.rem(me // bit + k // bit, 2)
        bit *= 2
    return out


def place(ids, me, n, capacity):
    t = ids.shape[1]
    onehot = lax.broadcasted_iota(jnp.int32, (n, t), 0) == ids
    before = lax.broadcasted_iota(jnp.int32, (t, t), 0) < lax.broadcasted_iota(jnp.int32, (t, t), 1)
    counts = jnp.dot(
        onehot.astype(F32).astype(BF16), before.astype(F32).astype(BF16), preferred_element_type=F32
    )
    rank = jnp.sum(jnp.where(onehot, counts, 0.0), axis=0, keepdims=True).astype(jnp.int32)
    return ids ^ me, rank, rank < capacity


def exchange_kernel(
    n, groups, capacity, pad, ids_hbm, gate_hbm, tokens_hbm, cot_hbm, wup_hbm, wdn_hbm,
    back_ref, up_out, down_out, pick_out,
    ids_ref, gate_ref, tokens_ref, cot_ref, scaled, wup, wdn, send, recv, ret, hg, a_all, hg_all,
    up_acc, down_acc, pick,
    in_sem, out_sem, send_sem, recv_sem, rsend_sem, rrecv_sem,
    asend_sem, arecv_sem, hsend_sem, hrecv_sem,
):
    dp = lax.axis_index("dp")
    me = lax.axis_index("expert")
    width = tokens_ref.shape[1]
    units = wup.shape[1]
    cols = width // groups
    chunks = n // CHUNK
    lead = chunks // 2 * CHUNK
    quarter = me // (n // 4)
    middle = (quarter == 1) | (quarter == 2)
    pairs = (
        (ids_hbm, ids_ref), (tokens_hbm, tokens_ref), (gate_hbm, gate_ref), (cot_hbm, cot_ref),
        (wup_hbm, wup), (wdn_hbm, wdn),
    )
    loads = [pltpu.make_async_copy(src, dst, in_sem.at[i]) for i, (src, dst) in enumerate(pairs)]
    for copy in loads[:4]:
        copy.start()

    barrier = pltpu.get_barrier_semaphore()

    @pl.loop(1, n)
    def _(k):
        pl.semaphore_signal(
            barrier, inc=1, device_id=(dp, partner(me, k, n)), device_id_type=MESH
        )

    @pl.loop(1, groups)
    def _(d):
        pl.semaphore_signal(
            barrier, inc=1, device_id=(lax.rem(dp + d, groups), me), device_id_type=MESH
        )

    loads[0].wait()
    offset, rank, kept = place(ids_ref[...], me, n, capacity)
    t = tokens_ref.shape[0]
    target = jnp.where(kept, offset * pad + rank, -1)
    rows = CHUNK * pad
    step = 512 if width % 512 == 0 else width
    for copy in loads[1:4]:
        copy.wait()
    for copy in loads[4:]:
        copy.start()
    scaled[...] = (column(gate_ref[...]) * cot_ref[...].astype(F32)).astype(BF16)

    def build(c):
        slot = lax.broadcasted_iota(jnp.int32, (rows, t), 0) + c * rows
        select = (slot == target).astype(F32).astype(BF16)
        for at in range(0, width, step):
            x = jnp.dot(select, tokens_ref[:, at : at + step], preferred_element_type=F32)
            y = jnp.dot(select, scaled[:, at : at + step], preferred_element_type=F32)
            both = jnp.concatenate([x.reshape(CHUNK, pad, step), y.reshape(CHUNK, pad, step)], axis=1)
            both = both.astype(BF16)
            send[pl.ds(c * CHUNK, CHUNK), :, at : at + step] = both
            if isinstance(c, int) and c == 0:
                recv[0, :, at : at + step] = both[0]

    build(chunks // 2)
    pl.semaphore_wait(barrier, n - 1 + groups - 1)

    def forth(k):
        return pltpu.make_async_remote_copy(
            src_ref=send.at[k], dst_ref=recv.at[k], send_sem=send_sem.at[k],
            recv_sem=recv_sem.at[k], device_id=(dp, partner(me, k, n)), device_id_type=MESH,
        )

    def home(k):
        return pltpu.make_async_remote_copy(
            src_ref=ret.at[k], dst_ref=back_ref.at[k], send_sem=rsend_sem.at[k],
            recv_sem=rrecv_sem.at[k], device_id=(dp, partner(me, k, n)), device_id_type=MESH,
        )

    def a_remote(c, d):
        peer = lax.rem(dp + d, groups)
        return pltpu.make_async_remote_copy(
            src_ref=recv.at[
                pl.ds(c * CHUNK, CHUNK), :, pl.ds(pl.multiple_of(peer * cols, 128), cols)
            ],
            dst_ref=a_all.at[d - 1, pl.ds(c * CHUNK, CHUNK)], send_sem=asend_sem.at[d - 1, c],
            recv_sem=arecv_sem.at[d - 1, c], device_id=(peer, me), device_id_type=MESH,
        )

    def h_remote(c, d):
        peer = lax.rem(dp + d, groups)
        return pltpu.make_async_remote_copy(
            src_ref=hg.at[pl.ds(c * CHUNK, CHUNK)],
            dst_ref=hg_all.at[d - 1, pl.ds(c * CHUNK, CHUNK)], send_sem=hsend_sem.at[d - 1, c],
            recv_sem=hrecv_sem.at[d - 1, c], device_id=(peer, me), device_id_type=MESH,
        )

    for k in range(lead, lead + CHUNK):
        forth(k).start()
    build(0)
    for k in range(1, CHUNK):
        forth(k).start()

    @pl.loop(1, chunks)
    def _(c):
        @pl.when(c != chunks // 2)
        def _():
            build(c)

    @pl.when(jnp.logical_not(middle))
    def _():
        for k in range(lead, lead + CHUNK // 2):
            forth(k).wait_send()

    @pl.loop(0, n - CHUNK)
    def _(i):
        k = n - 1 - i

        @pl.when((k < lead) | (k >= lead + CHUNK))
        def _():
            forth(k).start()

    for copy in loads[4:]:
        copy.wait()

    nt = (((1,), (1,)), ((), ()))

    def serve(c, m):
        count = m * CHUNK
        held = pl.ds(c * CHUNK, count)

        @pl.loop(0, count)
        def _(j):
            k = c * CHUNK + j

            @pl.when(k > 0)
            def _():
                forth(k).wait_recv()

        @pl.loop(1, groups)
        def _(d):
            for i in range(m):
                a_remote(c + i, d).start()

        a = recv[held].reshape(m * 2 * rows, width)
        pre = jnp.dot(a, wup[...], preferred_element_type=F32)
        grad = lax.dot_general(a, wdn[...], nt, preferred_element_type=F32)
        pre = pre.reshape(count, 2, pad, units)[:, 0]
        grad = grad.reshape(count, 2, pad, units)[:, 1]
        sigma = 1.0 / (1.0 + jnp.exp(-pre))
        hidden = pre * sigma
        grad = grad * sigma * (1.0 + pre * (1.0 - sigma))
        hg[held] = jnp.concatenate([grad, hidden], axis=1).astype(BF16)

        @pl.loop(1, groups)
        def _(d):
            for i in range(m):
                h_remote(c + i, d).start()

        hidden = hidden.reshape(m * rows, units).astype(BF16)
        grad = grad.reshape(m * rows, units).astype(BF16)
        for at in range(0, width, step):
            out = jnp.dot(hidden, wdn[:, at : at + step], preferred_element_type=F32)
            tok = lax.dot_general(grad, wup[at : at + step, :], nt, preferred_element_type=F32)
            both = jnp.concatenate(
                [tok.reshape(count, pad, step), out.reshape(count, pad, step)], axis=1
            )
            ret[held, :, at : at + step] = both.astype(BF16)

        @pl.loop(0, count)
        def _(j):
            k = c * CHUNK + j

            @pl.when(k > 0)
            def _():
                home(k).start()

    serve(chunks // 2, 1)
    serve(0, 2)

    @pl.loop(2, chunks)
    def _(c):
        @pl.when(c != chunks // 2)
        def _():
            serve(c, 1)

    slots = n * 2 * pad
    there = column(jnp.where(kept, offset * (2 * pad) + rank, -2 * pad))
    slot = lax.broadcasted_iota(jnp.int32, (t, slots), 1)
    pick[0] = (slot == there).astype(F32).astype(BF16)
    pick[1] = (slot == there + pad).astype(F32).astype(BF16)
    pick_copy = pltpu.make_async_copy(pick, pick_out, out_sem.at[0])
    pick_copy.start()

    own = pltpu.make_async_copy(ret.at[0], back_ref.at[0], out_sem.at[1])
    own.start()

    inverse = 1.0 / groups
    tile = 256 if cols % 256 == 0 else cols
    tn = (((0,), (0,)), ((), ()))

    def add_group(a_tile, grads, add):
        grads = grads.reshape(slots, units)
        first = lax.rem(lax.broadcasted_iota(jnp.int32, grads.shape, 0), 2 * pad) < pad
        zero = jnp.zeros_like(grads)
        grad = jnp.where(first, grads, zero)
        hidden = jnp.where(first, zero, grads)
        for at in range(0, cols, tile):
            a = a_tile(at).reshape(slots, tile)
            up = lax.dot_general(a, grad, tn, preferred_element_type=F32) * inverse
            down = lax.dot_general(hidden, a, tn, preferred_element_type=F32) * inverse
            if add:
                up += up_acc[at : at + tile, :]
                down += down_acc[:, at : at + tile]
            up_acc[at : at + tile, :] = up
            down_acc[:, at : at + tile] = down

    add_group(
        lambda at: recv[:, :, pl.ds(pl.multiple_of(dp * cols + at, 128), tile)], hg[...], False
    )

    @pl.loop(1, groups)
    def _(d):
        @pl.loop(0, chunks)
        def _(c):
            a_remote(c, d).wait_recv()
            h_remote(c, d).wait_recv()

        add_group(lambda at: a_all[d - 1, :, :, at : at + tile], hg_all[d - 1], True)

    up_copy = pltpu.make_async_copy(up_acc, up_out, out_sem.at[2])
    down_copy = pltpu.make_async_copy(down_acc, down_out, out_sem.at[3])
    up_copy.start()
    down_copy.start()

    @pl.loop(1, groups)
    def _(d):
        @pl.loop(0, chunks)
        def _(c):
            a_remote(c, d).wait_send()
            h_remote(c, d).wait_send()

    for copy in (pick_copy, own, up_copy, down_copy):
        copy.wait()

    @pl.loop(1, n)
    def _(k):
        @pl.when(middle | (k < lead) | (k >= lead + CHUNK // 2))
        def _():
            forth(k).wait_send()

        home(k).wait()


def nbytes(arrays):
    return sum(math.prod(shape) * jnp.dtype(kind).itemsize for shape, kind in arrays)


def exchange(n, groups, capacity, pad, ids, gate, tokens, cot, wup, wdn):
    t, width = tokens.shape
    units = wup.shape[1]
    cols = width // groups
    chunks = n // CHUNK
    hbm = pl.BlockSpec(memory_space=pltpu.HBM)
    anywhere = pl.BlockSpec(memory_space=pl.ANY)
    dma = pltpu.SemaphoreType.DMA
    block = (n, 2 * pad, width)
    buffers = [
        ((1, t), jnp.int32), ((1, t), F32), ((t, width), BF16), ((t, width), BF16),
        ((t, width), BF16), (wup.shape, BF16), (wdn.shape, BF16), (block, BF16), (block, BF16), (block, BF16),
        ((n, 2 * pad, units), BF16),
        ((groups - 1, n, 2 * pad, cols), BF16), ((groups - 1, n, 2 * pad, units), BF16),
        ((cols, units), F32), ((units, cols), F32), ((2, t, n * 2 * pad), BF16),
    ]
    results = [
        (block, BF16), ((cols, units), F32), ((units, cols), F32), ((2, t, n * 2 * pad), BF16),
    ]
    limit = nbytes(buffers) + 10 * 2**20
    near = limit + nbytes(results) < 52 * 2**20
    place_of = pltpu.VMEM if near else jax.ShapeDtypeStruct
    return pl.pallas_call(
        functools.partial(exchange_kernel, n, groups, capacity, pad),
        out_shape=tuple(place_of(shape, kind) for shape, kind in results),
        in_specs=[hbm] * 6,
        out_specs=(anywhere,) * 4,
        scratch_shapes=[pltpu.VMEM(shape, kind) for shape, kind in buffers]
        + [
            dma((6,)), dma((4,)), dma((n,)), dma((n,)), dma((n,)), dma((n,)),
            dma((groups - 1, chunks)), dma((groups - 1, chunks)),
            dma((groups - 1, chunks)), dma((groups - 1, chunks)),
        ],
        compiler_params=pltpu.CompilerParams(
            collective_id=0, has_side_effects=True, vmem_limit_bytes=limit
        ),
        name="expert_exchange",
    )(*(pltpu.with_memory_space_constraint(x, pltpu.HBM) for x in (ids, gate, tokens, cot, wup, wdn)))


def finish_kernel(
    gate_ref, pick_ref, back_ref, up_ref, down_ref, out_ref, tok_ref, up_out, down_out,
    out_buf, tok_buf, sem, row_sem,
):
    parts = sem.shape[1]
    copies = []
    for which, (src, dst) in enumerate(((up_ref, up_out), (down_ref, down_out))):
        size = src.shape[0] // parts
        for i in range(parts):
            rows = pl.ds(i * size, size)
            copies.append(pltpu.make_async_copy(src.at[rows], dst.at[rows], sem.at[which, i]))
    for copy in copies:
        copy.start()
    gate = column(gate_ref[...])
    width = out_ref.shape[1]
    step = 512 if width % 512 == 0 else width
    for i in range(width // step):
        at = pl.ds(i * step, step)
        rows = back_ref[:, at]
        tok = jnp.dot(pick_ref[0], rows, preferred_element_type=F32).astype(BF16)
        tok_buf[:, at] = tok
        out = jnp.dot(pick_ref[1], rows, preferred_element_type=F32)
        out_buf[:, at] = (gate * out).astype(BF16)
        for j, (src, dst) in enumerate(((tok_buf, tok_ref), (out_buf, out_ref))):
            copies.append(
                pltpu.make_async_copy(src.at[:, at], dst.at[:, at], row_sem.at[j, i])
            )
            copies[-1].start()
    for copy in copies:
        copy.wait()


def finish(gate, pick, back, up, down):
    t, width = gate.shape[1], back.shape[1]
    vmem = pl.BlockSpec(memory_space=pltpu.VMEM)
    anywhere = pl.BlockSpec(memory_space=pl.ANY)
    steps = width // 512 if width % 512 == 0 else 1
    return pl.pallas_call(
        finish_kernel,
        out_shape=(
            jax.ShapeDtypeStruct((t, width), BF16),
            jax.ShapeDtypeStruct((t, width), BF16),
            jax.ShapeDtypeStruct(up.shape, F32),
            jax.ShapeDtypeStruct(down.shape, F32),
        ),
        in_specs=[vmem, vmem, vmem, anywhere, anywhere],
        out_specs=(anywhere,) * 4,
        scratch_shapes=[
            pltpu.VMEM((t, width), BF16), pltpu.VMEM((t, width), BF16),
            pltpu.SemaphoreType.DMA((2, 4)), pltpu.SemaphoreType.DMA((2, steps)),
        ],
        compiler_params=pltpu.CompilerParams(vmem_limit_bytes=16 * 2**20),
        name="finish",
    )(gate, pick, back, up, down)


def shards(tokens, expert_ids, gate, cotangent, w_up, w_down):
    t = tokens.shape[0]
    n = lax.axis_size("expert")
    groups = lax.axis_size("dp")
    capacity = t // n
    pad = -(-capacity // 8) * 8
    gate = gate[None]
    back, up, down, pick = exchange(
        n, groups, capacity, pad, expert_ids[None], gate, tokens, cotangent, w_up[0], w_down[0]
    )
    out, tok, up, down = finish(gate, pick, back.reshape(n * 2 * pad, -1), up, down)
    return out, tok, up[None], down[None]


def solution(mesh):
    in_specs = (
        P(("dp", "expert"), None),
        P(("dp", "expert")),
        P(("dp", "expert")),
        P(("dp", "expert"), None),
        P("expert", None, None),
        P("expert", None, None),
    )
    out_specs = (
        P(("dp", "expert"), None),
        P(("dp", "expert"), None),
        P("expert", "dp", None),
        P("expert", None, "dp"),
    )
    return jax.shard_map(shards, mesh=mesh, in_specs=in_specs, out_specs=out_specs, check_vma=False)
```
